128 devices in a mesh: lat: 32 (over y, x, core), chan: 4 (over z).
Axes of the slice: x: 4, y: 4, z: 4, core: 2. Of those that a mesh axis runs over, the one named last changes fastest.
Arguments:
- fields: float32 [1, 256, 12, 28800], P(None, 'lat', 'chan'), may hold values from -1000 to 1000
- cotangent: float32 [1, 256, 12, 28800], P(None, 'lat', 'chan'), may hold values from -6 to 6
- norm_gain: float32 [768], P('chan'), may hold values from 0.1 to 1.9
- norm_shift: float32 [768], P('chan'), may hold values from -3 to 3
- first_weight: float32 [2, 8, 9216], P(None, 'chan'), may hold values from -0.4375 to 0.4375
- first_bias: float32 [2, 8, 96], P(None, 'chan'), may hold values from -3 to 3
- second_weight: float32 [2, 8, 9216], P(None, 'chan'), may hold values from -0.4375 to 0.4375
- second_bias: float32 [2, 8, 96], P(None, 'chan'), may hold values from -3 to 3
Outputs:
- mixed_field: float32 [1, 256, 12, 28800], P(None, 'lat', 'chan')
- grad_fields: float32 [1, 256, 12, 28800], P(None, 'lat', 'chan')
- grad_gain: float32 [768], P('chan')
- grad_shift: float32 [768], P('chan')
- grad_first_weight: float32 [2, 8, 9216], P(None, 'chan')
- grad_first_bias: float32 [2, 8, 96], P(None, 'chan')
- grad_second_weight: float32 [2, 8, 9216], P(None, 'chan')
- grad_second_bias: float32 [2, 8, 96], P(None, 'chan')
The draws below stay inside these ranges and needn't reach their ends.
All inputs are finite; a program needn't handle non-finite values.
Results may differ from the reference program's by a relative error of at most 0.0044.
Values sent between devices are 32-bit elements; how exact they have to be, the bound alone decides.
A program may use at most 128 MiB of HBM per device.

```python
import jax
import jax.numpy as jnp
from jax import lax

BATCH = 1
LON = 450
MODES = 224
EMBED = 768
BLOCKS = 8
CSUB = 64
BLOCK = 96
CGROUPS = 12
LAT = 256


def draw_fields(key, part):
    key = jax.random.fold_in(key, 7)
    base_key, row_key, channel_key, offset_key = jax.random.split(key, 4)
    target = (BATCH, LAT, LON, EMBED)
    row_shape = (BATCH, LAT, LON, 1)
    channel = jnp.arange(EMBED, dtype=jnp.float32) / EMBED
    random_base = jnp.clip(jax.random.normal(base_key, target, jnp.float32), -5.0, 5.0)
    row_log = jax.random.uniform(row_key, row_shape, jnp.float32, 0.0, 1.0)
    offset = jnp.clip(jax.random.normal(offset_key, row_shape, jnp.float32), -3.0, 3.0)
    channel_log = channel + 0.2 * jax.random.uniform(channel_key, (EMBED,), jnp.float32, -1.0, 1.0)
    values = 10.0 ** row_log * (offset + 10.0 ** channel_log * random_base)
    grouped = values.reshape(BATCH, LAT, LON, CGROUPS, CSUB).transpose(0, 1, 3, 2, 4)
    return grouped.reshape(BATCH, LAT, CGROUPS, LON * CSUB)


def block_scale(stream_key, dims, cuts, smallest, top_value):
    def one(dim, blocks):
        steps = jax.random.uniform(jax.random.fold_in(jax.random.fold_in(stream_key, 6), dim), (blocks,), jnp.float32, smallest / len(cuts), top_value / len(cuts))
        return jnp.repeat(jnp.exp(steps), dims[dim] // blocks).reshape((-1,) + (1,) * (len(dims) - dim - 1))

    factor_of = one(*cuts[0])
    for cut in cuts[1:]:
        factor_of = factor_of * one(*cut)
    return factor_of


def scatter_about(rng, dims, scale, bound, shards=(), kind=jnp.bfloat16):
    loudness = block_scale(rng, dims, shards, -0.22, 0.18) if shards else 1.0
    values = jax.random.normal(rng, dims, jnp.float32) * scale * loudness
    return jnp.minimum(jnp.maximum(values, -bound), bound).astype(kind)


def setup_inputs(seed: int = 0) -> dict:
    streams_of = jax.random.split(jax.random.key(seed), 9)
    return {
        "fields": draw_fields(jax.random.fold_in(streams_of[8], 71), 0),
        "cotangent": scatter_about(streams_of[1], (BATCH, LAT, CGROUPS, LON * CSUB), 1.0, 6.0, ((1, 32), (2, 4)), jnp.float32),
        "norm_gain": jnp.clip(1.0 + 0.18 * jax.random.normal(streams_of[2], (EMBED,), jnp.float32), 0.1, 1.9),
        "norm_shift": scatter_about(streams_of[3], (EMBED,), 0.5, 3.0, ((0, 4),), jnp.float32),
        "first_weight": scatter_about(streams_of[4], (2, BLOCKS, BLOCK * BLOCK), (2 * BLOCK) ** -0.5, 0.4375, ((1, 4),), jnp.float32),
        "first_bias": scatter_about(streams_of[5], (2, BLOCKS, BLOCK), 0.5, 3.0, ((1, 4),), jnp.float32),
        "second_weight": scatter_about(streams_of[6], (2, BLOCKS, BLOCK * BLOCK), (2 * BLOCK) ** -0.5, 0.4375, ((1, 4),), jnp.float32),
        "second_bias": scatter_about(streams_of[7], (2, BLOCKS, BLOCK), 0.5, 3.0, ((1, 4),), jnp.float32),
    }


epsilon = 1e-05
shrink_level = 0.05

def to_tokens(stored):
    samples, rows, groups, flat = stored.shape
    width = flat // LON
    return stored.reshape(samples, rows, groups, LON, width).transpose(0, 1, 3, 2, 4).reshape(samples, rows, LON, groups * width)

def from_tokens(values):
    samples, rows, lon_count, channels = values.shape
    groups = channels // CSUB
    return values.reshape(samples, rows, lon_count, groups, CSUB).transpose(0, 1, 3, 2, 4).reshape(samples, rows, groups, lon_count * CSUB)

def complex_apply(real_part, imag_part, weights):
    high = lax.Precision.HIGHEST
    first = jnp.einsum('abcki,kio->abcko', real_part, weights[0], precision=high)
    second = jnp.einsum('abcki,kio->abcko', imag_part, weights[1], precision=high)
    third = jnp.einsum('abcki,kio->abcko', imag_part, weights[0], precision=high)
    fourth = jnp.einsum('abcki,kio->abcko', real_part, weights[1], precision=high)
    return (first - second, third + fourth)

def afno_layer(fields, norm_gain, norm_shift, first_weight, first_bias, second_weight, second_bias):
    average = lax.optimization_barrier(jnp.mean(fields, -1, keepdims=True))
    centred = fields - average
    variance = lax.optimization_barrier(jnp.mean(centred * centred, -1, keepdims=True))
    normed = centred * lax.rsqrt(variance + epsilon) * norm_gain + norm_shift
    spectrum = jnp.fft.rfft2(normed, axes=(1, 2), norm='ortho')[:, :, :MODES, :]
    target = spectrum.shape[:-1] + (BLOCKS, BLOCK)
    real_in = jnp.real(spectrum).reshape(target)
    imag_in = jnp.imag(spectrum).reshape(target)
    pre_real, pre_imag = complex_apply(real_in, imag_in, first_weight)
    act_real = jax.nn.relu(pre_real + first_bias[0])
    act_imag = jax.nn.relu(pre_imag + first_bias[1])
    out_real, out_imag = complex_apply(act_real, act_imag, second_weight)
    out_real = out_real + second_bias[0]
    out_imag = out_imag + second_bias[1]
    out_real = out_real - jnp.clip(out_real, -shrink_level, shrink_level)
    out_imag = out_imag - jnp.clip(out_imag, -shrink_level, shrink_level)
    shrunk = lax.complex(out_real, out_imag).reshape(spectrum.shape)
    padded = jnp.pad(shrunk, ((0, 0), (0, 0), (0, LON // 2 + 1 - MODES), (0, 0)))
    filtered = jnp.fft.irfft2(padded, s=(LAT, LON), axes=(1, 2), norm='ortho')
    return normed + filtered

def reference(fields, cotangent, norm_gain, norm_shift, first_weight, first_bias, second_weight, second_bias):
    tokens = to_tokens(fields)
    upstream = to_tokens(cotangent)
    square = (2, BLOCKS, BLOCK, BLOCK)
    flat = (2, BLOCKS, BLOCK * BLOCK)
    mixed, pullback = jax.vjp(afno_layer, tokens, norm_gain, norm_shift, first_weight.reshape(square), first_bias, second_weight.reshape(square), second_bias)
    gradients = pullback(upstream)
    factor = (BATCH * LAT * LON) ** (-0.5)
    return (from_tokens(mixed), from_tokens(gradients[0]), gradients[1] * factor, gradients[2] * factor, gradients[3].reshape(flat) * factor, gradients[4] * factor, gradients[5].reshape(flat) * factor, gradients[6] * factor)
```

```python
import functools
import math

import jax
import jax.numpy as jnp
import ml_dtypes
import numpy as np
from jax import lax
from jax.experimental import pallas as pl
from jax.experimental.pallas import tpu as pltpu
from jax.sharding import PartitionSpec as P

F32 = jnp.float32
BF16 = jnp.bfloat16
MESH = pl.DeviceIdType.MESH

LON = 450
EMBED = 768
LOCAL = 192
BLOCK = 96
PAIRS = 225
PADDED = 240
STRIP = PADDED * 8
REAL = PAIRS * 8
RANK = 112
TALL = 120
OWN = 7
KINDS = 3
CHUNK = OWN * KINDS * 8
PIECE = 384
GRAD_ROWS = 104
PART = 32
PARTS = 4 * GRAD_ROWS // PART

epsilon = 1e-05
shrink_level = 0.05

SIX = ((1, 1), (0, 2), (2, 0), (0, 1), (1, 0), (0, 0))
THREE = ((0, 1), (1, 0), (0, 0))
FACTOR = 1.0 / math.sqrt(256 * LON)


def split_table(values, count):
    parts = []
    rest = values.astype(np.float64)
    for _ in range(count):
        part = rest.astype(np.float32).astype(ml_dtypes.bfloat16)
        parts.append(part)
        rest = rest - part.astype(np.float64)
    return np.stack(parts)


def make_tables():
    order = np.array([0] + list(range(2, 113)) + [1])
    places = np.arange(PAIRS)
    angles = 2.0 * np.pi * (order[:, None] * places[None, :] % PAIRS) / PAIRS
    plain = np.zeros((PADDED, PADDED))
    plain[: len(order), :PAIRS] = np.cos(angles) / np.sqrt(LON)
    plain[TALL : TALL + len(order), :PAIRS] = -np.sin(angles) / np.sqrt(LON)
    scale = np.full(TALL, 2.0)
    scale[0] = 1.0
    double = plain * np.concatenate([scale, scale])[:, None]
    turn = np.zeros((2, TALL, 128), np.float32)
    turn[0, :, :64] = 1.0
    turn[0, : len(order), 64:] = np.cos(2.0 * np.pi * order / LON)[:, None]
    turn[1, : len(order), 64:] = np.sin(2.0 * np.pi * order / LON)[:, None]
    rows = np.arange(256)
    lat_angles = 2.0 * np.pi * (rows[:, None] * rows[None, :] % 256) / 256
    lat = np.concatenate([np.cos(lat_angles), np.sin(lat_angles)]) / 16.0
    place = np.zeros((2, 2, 2, 128, 256), np.float32)
    for core in range(2):
        for mode in range(2):
            for part in range(2):
                for i in range(BLOCK):
                    in_shared = i >= 64 if core == 0 else i < 32
                    if in_shared:
                        lane = 128 + 64 * part + 32 * mode + i % 32
                    else:
                        lane = 64 * part + (i if core == 0 else i - 32)
                    place[core, mode, part, i, lane] = 1.0
    halves = np.zeros((2, 8, 128), np.float32)
    halves[0, 0, :64] = 1.0
    halves[0, 1, 64:] = 1.0
    halves[1, 2, :64] = 1.0
    halves[1, 3, 64:] = 1.0
    bf = ml_dtypes.bfloat16
    return (
        split_table(plain, 3),
        split_table(double, 2),
        split_table(plain.T, 2),
        split_table(double.T, 2),
        split_table(lat, 3),
        turn,
        place.astype(bf),
        np.swapaxes(place, -1, -2).astype(bf),
        halves,
    )


def split(value, count):
    parts = []
    for _ in range(count):
        part = value.astype(BF16)
        parts.append(part)
        value = value - part.astype(F32)
    return parts


def dots(left, right, pairs, dims=((1,), (0,))):
    total = None
    for i, j in pairs:
        term = lax.dot_general(left[i], right[j], (dims, ((), ())), preferred_element_type=F32)
        total = term if total is None else total + term
    return total


def kernel(
    fields,
    cotangent,
    norm,
    weights,
    plain,
    double,
    back_plain,
    back_double,
    lat_table,
    turn,
    place,
    place_t,
    halves,
    mixed_out,
    grad_out,
    param_out,
    norm_out,
    scaled,
    cot,
    inv,
    result,
    send1,
    send2,
    send3,
    send4,
    recv1,
    recv2,
    recv3,
    recv4,
    mid1,
    mid2,
    mid3,
    mid4,
    act,
    shrunk,
    mats,
    mats_grad,
    sums_grad,
    bias,
    zsend,
    zrecv,
    part_send,
    part_recv,
    part_sum,
    norm_send,
    norm_recv,
    io_sem,
    z_ssem,
    z_rsem,
    s_sem,
    r_sem,
    m_sem,
    p_ssem,
    p_rsem,
    g_ssem,
    g_rsem,
    n_ssem,
    n_rsem,
):
    me = lax.axis_index("lat")
    zed = lax.axis_index("chan")
    y, x, core = me // 8, (me // 2) % 4, me % 2
    chip = y * 4 + x
    lane = lax.broadcasted_iota(jnp.int32, (1, 128), 1)
    low = lane < 64
    low32 = lane % 64 < 32
    sign = jnp.where(low, 1.0, -1.0).astype(F32)

    sends = (send1, send2, send3, send4)
    recvs = (recv1, recv2, recv3, recv4)
    mids = (mid1, mid2, mid3, mid4)

    def at(dy, dx):
        return lax.rem(y + dy, 4), lax.rem(x + dx, 4)

    def index(row, column, half):
        return (row * 4 + column) * 2 + half

    def row_slot(row, column, half):
        return half * 16 + row * 4 + column

    def slots(n):
        return (row_slot, index) if n < 2 else (index, row_slot)

    direct = [(0, 0, 2)] + [(0, d, k) for d in (1, 3, 2) for k in (0, 1)]
    direct += [(d, 0, k) for d in (1, 3, 2) for k in (0, 1)]
    corner = [(dy, dx, k) for dy in (1, 3, 2) for dx in (1, 3, 2) for k in (0, 1)]

    def corner_slot(dy, dx, k):
        return k * 9 + (dy - 1) * 3 + dx - 1

    def remote(src, dst, ssem, rsem, device):
        return pltpu.make_async_remote_copy(
            src_ref=src,
            dst_ref=dst,
            send_sem=ssem,
            recv_sem=rsem,
            device_id=(device, zed),
            device_id_type=MESH,
        )

    def first_leg(n, i):
        dy, dx, k = corner[i]
        row, column = at(dy, dx)
        src_slot = slots(n)[0](row, column, k)
        slot = corner_slot(dy, dx, k)
        device = index(y, column, core) if k == 0 else index(row, x, core)
        return remote(
            sends[n].at[src_slot], mids[n].at[slot], s_sem.at[n, i], m_sem.at[n, slot], device
        )

    def second_leg(n, i):
        dy, dx, k = corner[i]
        slot = corner_slot(dy, dx, k)
        if k == 0:
            origin = (y, lax.rem(x + 4 - dx, 4))
            final = (lax.rem(y + dy, 4), x)
        else:
            origin = (lax.rem(y + 4 - dy, 4), x)
            final = (y, lax.rem(x + dx, 4))
        return remote(
            mids[n].at[slot],
            recvs[n].at[slots(n)[1](origin[0], origin[1], core)],
            s_sem.at[n, 18 + i],
            r_sem.at[n, index(origin[0], origin[1], core)],
            index(final[0], final[1], k),
        )

    def direct_leg(n, i):
        dy, dx, k = direct[i]
        half = 1 - core if k == 2 else k
        row, column = at(dy, dx)
        return remote(
            sends[n].at[slots(n)[0](row, column, half)],
            recvs[n].at[slots(n)[1](y, x, core)],
            s_sem.at[n, 36 + i],
            r_sem.at[n, me],
            index(row, column, half),
        )

    def start(n):
        for i in range(18):
            first_leg(n, i).start()
        for i in range(13):
            direct_leg(n, i).start()
        mine = slots(n)[0](y, x, core)
        theirs = slots(n)[1](y, x, core)
        recvs[n][theirs] = sends[n][mine]

    def forward(n):
        for i in range(18):
            first_leg(n, i).wait_recv()
            second_leg(n, i).start()

    def finish(n):
        for d in range(1, 32):
            origin = lax.rem(me + d, 32)
            slot = slots(n)[1](origin // 8, (origin // 2) % 4, origin % 2)
            remote(
                sends[n].at[0], recvs[n].at[slot], s_sem.at[n, 0], r_sem.at[n, origin], origin
            ).wait_recv()

    def drain(n):
        for i in range(18):
            first_leg(n, i).wait_send()
            second_leg(n, i).wait_send()
        for i in range(13):
            direct_leg(n, i).wait_send()

    def exchange(stage):
        copies = []
        for d in range(1, 4):
            other = lax.rem(zed + d, 4)
            copies.append(
                pltpu.make_async_remote_copy(
                    src_ref=zsend.at[stage],
                    dst_ref=zrecv.at[stage, zed],
                    send_sem=z_ssem.at[stage, d],
                    recv_sem=z_rsem.at[stage, zed],
                    device_id=(me, other),
                    device_id_type=MESH,
                )
            )
        for copy in copies:
            copy.start()
        zrecv[stage, zed] = zsend[stage]
        return copies

    def exchange_wait(stage, copies):
        for copy in copies:
            copy.wait_send()
        for d in range(1, 4):
            other = lax.rem(zed + d, 4)
            pltpu.make_async_remote_copy(
                src_ref=zsend.at[stage],
                dst_ref=zrecv.at[stage, other],
                send_sem=z_ssem.at[stage, d],
                recv_sem=z_rsem.at[stage, other],
                device_id=(me, other),
                device_id_type=MESH,
            ).wait_recv()

    def token_sums(value, which, count=3):
        pattern = halves[which].astype(BF16)
        total = None
        for part in reversed(split(value, count)):
            term = lax.dot_general(
                pattern, part, (((1,), (1,)), ((), ())), preferred_element_type=F32
            )
            total = term if total is None else total + term
        return total

    def spread(rows, which):
        return lax.dot_general(
            rows,
            halves[which],
            (((0,), (0,)), ((), ())),
            precision=lax.Precision.HIGHEST,
            preferred_element_type=F32,
        )

    def lon_forward(load, table, pairs, out):
        count = 3 if pairs is SIX else 2
        flat = out.reshape(32 * CHUNK, 128)
        cos_turn, sin_turn = turn[0], turn[1]
        top = lax.broadcasted_iota(jnp.int32, (TALL, 128), 0) == 0
        for g in range(3):

            def body(step, carry, g=g):
                h0 = step * 2
                data = jnp.concatenate([load(g, h0), load(g, h0 + 1)], axis=1)
                parts = split(data, count)
                both = dots([table[i] for i in range(count)], parts, pairs)
                for e in range(2):
                    real = both[:TALL, 128 * e : 128 * e + 128]
                    imag = both[TALL:, 128 * e : 128 * e + 128]
                    turned_real = real * cos_turn + imag * sin_turn
                    turned_imag = imag * cos_turn - real * sin_turn
                    even = jnp.where(low, turned_real, pltpu.roll(turned_imag, 64, 1))
                    odd = jnp.where(low, pltpu.roll(turned_real, 64, 1), turned_imag)
                    a = even + odd
                    b = (even - odd) * sign
                    b = jnp.where(top, a[RANK : RANK + 1], b)
                    h = h0 + e

                    def store(half, kind, value):
                        flat[pl.ds(half * 16 * CHUNK + kind * 8 + h, RANK, stride=24), :] = value[
                            :RANK
                        ]

                    if g == 1:
                        store(0, 2, jnp.where(low32, a, pltpu.roll(b, 32, 1)))
                        store(1, 2, jnp.where(low32, pltpu.roll(a, 96, 1), b))
                    else:
                        store(g // 2, 0, a)
                        store(g // 2, 1, b)
                return carry

            lax.fori_loop(0, 4, body, 0)

    def lon_inverse(source, table):
        flat = source.reshape(32 * CHUNK, 128)
        cos_turn, sin_turn = turn[0], turn[1]
        top = lax.broadcasted_iota(jnp.int32, (RANK, 128), 0) == 0
        top8 = lax.broadcasted_iota(jnp.int32, (8, 128), 0) == 0
        for g in range(3):

            def body(step, carry, g=g):
                h0 = step * 2
                columns = []
                for e in range(2):
                    h = h0 + e

                    def fetch(half, kind):
                        return flat[pl.ds(half * 16 * CHUNK + kind * 8 + h, RANK, stride=24), :]

                    if g == 1:
                        u0, u1 = fetch(0, 2), fetch(1, 2)
                        a = jnp.where(low32, u0, pltpu.roll(u1, 32, 1))
                        b = jnp.where(low32, pltpu.roll(u0, 96, 1), u1)
                    else:
                        a, b = fetch(g // 2, 0), fetch(g // 2, 1)
                    last = jnp.where(top8, b[0:1], 0.0)
                    b = jnp.where(top, 0.0, b * sign)
                    even = jnp.concatenate([a + b, last], axis=0)
                    odd = jnp.concatenate([a - b, last], axis=0)
                    real = jnp.where(low, even, pltpu.roll(odd, 64, 1))
                    imag = jnp.where(low, pltpu.roll(even, 64, 1), odd)
                    turned_real = real * cos_turn - imag * sin_turn
                    turned_imag = imag * cos_turn + real * sin_turn
                    columns.append(jnp.concatenate([turned_real, turned_imag], axis=0))
                data = jnp.concatenate(columns, axis=1)
                out = dots([table[0], table[1]], split(data, 2), THREE)
                for e in range(2):
                    result[pl.ds(g * STRIP + h0 + e, PADDED, stride=8), :] = out[
                        :, 128 * e : 128 * e + 128
                    ]
                return carry

            lax.fori_loop(0, 4, body, 0)

    def piece(ref, r, kind):
        return ref[:, pl.ds(pl.multiple_of(r * 24 + kind * 8, 8), 8), :].reshape(256, 128)

    def put(ref, r, kind, value):
        ref[:, pl.ds(pl.multiple_of(r * 24 + kind * 8, 8), 8), :] = value.reshape(32, 8, 128)

    def lat_mix(pieces, orient, pairs):
        count = 3 if pairs is SIX else 2
        data = jnp.concatenate(pieces, axis=1)
        both = dots([lat_table[i] for i in range(count)], split(data, count), pairs)
        out = []
        for kind in range(3):
            direct_part = both[:256, 128 * kind : 128 * kind + 128]
            turned = both[256:, 128 * kind : 128 * kind + 128]
            out.append(direct_part + (orient * sign) * pltpu.roll(turned, 64, 1))
        return out

    def apply(pieces, layer, pairs, transposed):
        count = 3 if pairs is SIX else 2
        dims = ((1,), (1,)) if transposed else ((1,), (0,))
        parts = [split(value, count) for value in pieces]
        out = []
        for mode in range(2):
            left = [
                jnp.concatenate([parts[mode][i], parts[2][i]], axis=1) for i in range(count)
            ]
            right = [mats[layer * 2 + mode, i] for i in range(count)]
            out.append(dots(left, right, pairs, dims))
        return [out[0][:, :128], out[1][:, :128], out[0][:, 128:] + out[1][:, 128:]]

    def mat_grad(inputs, outputs, layer):
        left = [split(value, 2) for value in inputs]
        right = [split(value, 2) for value in outputs]
        for mode in range(2):
            lhs = [jnp.concatenate([left[mode][i], left[2][i]], axis=1) for i in range(2)]
            rhs = [jnp.concatenate([right[mode][i], right[2][i]], axis=1) for i in range(2)]
            mats_grad[layer * 2 + mode] += dots(lhs, rhs, THREE, ((0,), (0,)))
            total = jnp.concatenate([outputs[mode], outputs[2]], axis=1)
            sums_grad[layer * 2 + mode] += jnp.sum(total.reshape(32, 8, 256), axis=0)

    loads = []
    for g in range(3):
        loads.append(
            pltpu.make_async_copy(
                cotangent.at[g], cot.at[pl.ds(g * STRIP, REAL)], io_sem.at[g]
            )
        )
    for g in range(3):
        loads.append(
            pltpu.make_async_copy(
                fields.at[g], scaled.at[pl.ds(g * STRIP, REAL)], io_sem.at[3 + g]
            )
        )
    for copy in loads:
        copy.start()
    barrier = pltpu.get_barrier_semaphore()
    for d in range(1, 32):
        pl.semaphore_signal(
            barrier, inc=1, device_id=(lax.rem(me + d, 32), zed), device_id_type=MESH
        )
    for d in range(1, 4):
        pl.semaphore_signal(
            barrier, inc=1, device_id=(me, lax.rem(zed + d, 4)), device_id_type=MESH
        )
    for g in range(3):
        cot[pl.ds(g * STRIP + REAL, STRIP - REAL), :] = jnp.zeros((STRIP - REAL, 128), F32)
        scaled[pl.ds(g * STRIP + REAL, STRIP - REAL), :] = jnp.zeros((STRIP - REAL, 128), F32)
    for copy in loads[:3]:
        copy.wait()

    def load_cot(g, h):
        return cot[pl.ds(g * STRIP + h, PADDED, stride=8), :]

    lon_forward(load_cot, double, THREE, send2)
    pl.semaphore_wait(barrier, 34)
    start(1)

    for copy in loads[3:]:
        copy.wait()
    for k in range(STRIP // PIECE):
        rows = [scaled[pl.ds(g * STRIP + k * PIECE, PIECE), :] for g in range(3)]
        here = token_sums(rows[0] + rows[1] + rows[2], 0)
        mean = spread(here * (1.0 / LOCAL), 0)
        square = None
        for value in rows:
            centred = value - mean
            square = centred * centred if square is None else square + centred * centred
        zsend[0, :, pl.ds(k * PIECE, PIECE)] = here + token_sums(square, 1)
    copies = exchange(0)
    exchange_wait(0, copies)
    row8 = lax.broadcasted_iota(jnp.int32, (8, PIECE), 0)
    for k in range(STRIP // PIECE):
        group = [zrecv[0, i, :, pl.ds(k * PIECE, PIECE)] for i in range(4)]
        total = (group[0] + group[1]) + (group[2] + group[3])
        mean = total * (1.0 / EMBED)
        apart = None
        for value in group:
            gap = value * (1.0 / LOCAL) - mean
            apart = gap * gap if apart is None else apart + gap * gap
        variance = (total + pltpu.roll(apart, 2, 0) * LOCAL) * (1.0 / EMBED)
        both = jnp.where(row8 < 2, mean, lax.rsqrt(jnp.maximum(variance, 0.0) + epsilon))
        mean = spread(both, 0)
        inverse = spread(both, 1)
        inv[pl.ds(k * PIECE, PIECE), :] = inverse
        for g in range(3):
            here = pl.ds(g * STRIP + k * PIECE, PIECE)
            scaled[here, :] = (scaled[here, :] - mean) * inverse

    def load_normed(g, h):
        value = scaled[pl.ds(g * STRIP + h, PADDED, stride=8), :]
        return value * norm[g : g + 1] + norm[3 + g : 4 + g]

    lon_forward(load_normed, plain, SIX, send1)
    start(0)
    forward(1)

    for layer in range(2):
        for mode in range(2):
            to_real, to_imag = place[core, mode, 0], place[core, mode, 1]
            real = split(weights[layer, 0, core], 3)
            imag = split(weights[layer, 1, core], 3)

            def fan(parts, target):
                total = None
                for part in reversed(parts):
                    term = jnp.dot(part, target, preferred_element_type=F32)
                    total = term if total is None else total + term
                return total

            upper = fan(real, to_real) + fan(imag, to_imag)
            lower = fan(real, to_imag) - fan(imag, to_real)
            bias[layer * 2 + mode] = jnp.broadcast_to(upper[BLOCK : BLOCK + 1], (8, 256))

            def lift(source, value):
                total = None
                for part in reversed(split(value, 3)):
                    term = jnp.dot(source, part, preferred_element_type=F32)
                    total = term if total is None else total + term
                return total

            whole = lift(place_t[core, mode, 0], upper) + lift(place_t[core, mode, 1], lower)
            for i, part in enumerate(split(whole, 3)):
                mats[layer * 2 + mode, i] = part

    def add_bias(pieces, layer):
        first, second = bias[layer * 2], bias[layer * 2 + 1]
        return [
            pieces[0] + first[0:1, :128],
            pieces[1] + second[0:1, :128],
            pieces[2] + (first[0:1, 128:] + second[0:1, 128:]),
        ]

    finish(1)

    def upstream_body(r, carry):
        out = lat_mix([piece(recv2, r, kind) for kind in range(3)], 1.0, THREE)
        for kind in range(3):
            put(recv2, r, kind, out[kind])
        return carry

    lax.fori_loop(0, OWN, upstream_body, 0)
    forward(0)
    finish(0)

    def forward_body(r, carry):
        spectrum = lat_mix([piece(recv1, r, kind) for kind in range(3)], 1.0, SIX)
        for kind in range(3):
            put(recv1, r, kind, spectrum[kind])
        hidden = [jnp.maximum(v, 0.0) for v in add_bias(apply(spectrum, 0, SIX, False), 0)]
        for kind in range(3):
            put(act, r, kind, hidden[kind])
        out = add_bias(apply(hidden, 1, SIX, False), 1)
        out = [v - jnp.clip(v, -shrink_level, shrink_level) for v in out]
        for kind in range(3):
            put(shrunk, r, kind, out[kind])
        rows = lat_mix(out, -1.0, THREE)
        for kind in range(3):
            put(send3, r, kind, rows[kind])
        return carry

    lax.fori_loop(0, OWN, forward_body, 0)
    start(2)

    mats_grad[...] = jnp.zeros_like(mats_grad)
    sums_grad[...] = jnp.zeros_like(sums_grad)

    def backward_body(r, carry):
        out_grad = [
            jnp.where(piece(shrunk, r, kind) != 0.0, piece(recv2, r, kind), 0.0)
            for kind in range(3)
        ]
        hidden = [piece(act, r, kind) for kind in range(3)]
        mat_grad(hidden, out_grad, 1)
        hidden_grad = apply(out_grad, 1, THREE, True)
        pre_grad = [jnp.where(h > 0.0, g, 0.0) for h, g in zip(hidden, hidden_grad)]
        mat_grad([piece(recv1, r, kind) for kind in range(3)], pre_grad, 0)
        rows = lat_mix(apply(pre_grad, 0, THREE, True), -1.0, THREE)
        for kind in range(3):
            put(send4, r, kind, rows[kind])
        return carry

    lax.fori_loop(0, OWN, backward_body, 0)

    bias_row = lax.broadcasted_iota(jnp.int32, (128, 128), 0) == BLOCK
    for layer in range(2):
        real_total, imag_total = None, None
        for mode in range(2):
            real_t, imag_t = place_t[core, mode, 0], place_t[core, mode, 1]
            real_p, imag_p = place[core, mode, 0], place[core, mode, 1]
            grads = split(mats_grad[layer * 2 + mode], 2)
            to_real = sum(jnp.dot(v, real_t, preferred_element_type=F32) for v in grads)
            to_imag = sum(jnp.dot(v, imag_t, preferred_element_type=F32) for v in grads)

            def lower_to(target, value):
                return sum(
                    jnp.dot(target, v, preferred_element_type=F32) for v in split(value, 2)
                )

            real = lower_to(real_p, to_real) + lower_to(imag_p, to_imag)
            imag = lower_to(real_p, to_imag) - lower_to(imag_p, to_real)
            column = jnp.sum(sums_grad[layer * 2 + mode], axis=0, keepdims=True)
            column = jnp.broadcast_to(column, (16, 256))
            sums = split(column, 3)
            real_bias = sum(jnp.dot(v, real_t, preferred_element_type=F32) for v in sums)
            imag_bias = sum(jnp.dot(v, imag_t, preferred_element_type=F32) for v in sums)
            real = jnp.where(bias_row, real_bias[0:1], real)
            imag = jnp.where(bias_row, imag_bias[0:1], imag)
            real_total = real if real_total is None else real_total + real
            imag_total = imag if imag_total is None else imag_total + imag
        part_send[pl.ds(layer * 2 * GRAD_ROWS, GRAD_ROWS), :] = real_total[:GRAD_ROWS]
        part_send[pl.ds((layer * 2 + 1) * GRAD_ROWS, GRAD_ROWS), :] = imag_total[:GRAD_ROWS]

    def part_copy(d):
        other = lax.rem(chip + d, 16)
        return other, remote(
            part_send.at[pl.ds(lax.rem(other, PARTS) * PART, PART)],
            part_recv.at[chip],
            p_ssem.at[d],
            p_rsem.at[chip],
            other * 2 + core,
        )

    for d in range(1, 16):
        other, copy = part_copy(d)
        pl.when(other < PARTS)(copy.start)
    part_recv[chip] = part_send[pl.ds(lax.rem(chip, PARTS) * PART, PART), :]
    start(3)
    forward(2)

    owner = chip < PARTS

    def sum_copy(d):
        other = lax.rem(me + d, 32)
        return other, remote(
            part_sum,
            param_out.at[core, pl.ds(lax.rem(chip, PARTS) * PART, PART)],
            g_ssem.at[d],
            g_rsem.at[me],
            other,
        )

    @pl.when(owner)
    def _():
        for d in range(1, 16):
            other = lax.rem(chip + d, 16)
            remote(
                part_send.at[pl.ds(0, PART)],
                part_recv.at[other],
                p_ssem.at[d],
                p_rsem.at[other],
                other * 2 + core,
            ).wait_recv()
        total = part_recv[0]
        for i in range(1, 16):
            total = total + part_recv[i]
        part_sum[...] = total * FACTOR
        param_out[core, pl.ds(lax.rem(chip, PARTS) * PART, PART), :] = total * FACTOR
        for d in range(1, 32):
            sum_copy(d)[1].start()

    finish(2)
    lon_inverse(recv3, back_double)
    for g in range(3):
        here = pl.ds(g * STRIP, REAL)
        result[here, :] = (
            result[here, :] + scaled[here, :] * norm[g : g + 1] + norm[3 + g : 4 + g]
        )
    stores = []
    for g in range(3):
        stores.append(
            pltpu.make_async_copy(
                result.at[pl.ds(g * STRIP, REAL)], mixed_out.at[g], io_sem.at[g]
            )
        )
        stores[-1].start()
    forward(3)
    for copy in stores:
        copy.wait()
    finish(3)

    lon_inverse(recv4, back_plain)
    gains = [None] * 6
    for k in range(STRIP // PIECE):
        direct_sum, cross_sum = None, None
        for g in range(3):
            here = pl.ds(g * STRIP + k * PIECE, PIECE)
            normed_grad = cot[here, :] + result[here, :]
            unit = scaled[here, :]
            for slot, value in ((g, normed_grad * unit), (3 + g, normed_grad)):
                value = jnp.sum(value.reshape(PIECE // 8, 8, 128), axis=0)
                gains[slot] = value if gains[slot] is None else gains[slot] + value
            scaled_grad = normed_grad * norm[g : g + 1]
            cot[here, :] = scaled_grad
            cross = scaled_grad * unit
            direct_sum = scaled_grad if direct_sum is None else direct_sum + scaled_grad
            cross_sum = cross if cross_sum is None else cross_sum + cross
        zsend[1, :, pl.ds(k * PIECE, PIECE)] = token_sums(direct_sum, 0) + token_sums(
            cross_sum, 1
        )
    copies = exchange(1)
    norm_rows = lax.broadcasted_iota(jnp.int32, (8, 128), 0)
    packed = jnp.zeros((8, 128), F32)
    for i, value in enumerate(gains):
        value = jnp.sum(value, axis=0, keepdims=True)
        packed = jnp.where(norm_rows == i, value, packed)
    norm_send[...] = packed + pltpu.roll(packed, 64, 1)
    norm_recv[me] = norm_send[...]

    def norm_copy(d):
        other = lax.rem(me + d, 32)
        return remote(norm_send, norm_recv.at[me], n_ssem.at[d], n_rsem.at[me], other)

    for d in range(1, 32):
        norm_copy(d).start()
    exchange_wait(1, copies)
    for k in range(STRIP // PIECE):
        group = [zrecv[1, i, :, pl.ds(k * PIECE, PIECE)] for i in range(4)]
        total = ((group[0] + group[1]) + (group[2] + group[3])) * (1.0 / EMBED)
        direct_mean = spread(total, 0)
        cross_mean = spread(total, 1)
        inverse = inv[pl.ds(k * PIECE, PIECE), :]
        for g in range(3):
            here = pl.ds(g * STRIP + k * PIECE, PIECE)
            cot[here, :] = inverse * (cot[here, :] - direct_mean - scaled[here, :] * cross_mean)
    stores = []
    for g in range(3):
        stores.append(
            pltpu.make_async_copy(
                cot.at[pl.ds(g * STRIP, REAL)], grad_out.at[g], io_sem.at[3 + g]
            )
        )
        stores[-1].start()

    for d in range(1, 32):
        other = lax.rem(me + d, 32)
        remote(
            norm_send, norm_recv.at[other], n_ssem.at[d], n_rsem.at[other], other
        ).wait_recv()
        norm_copy(d).wait_send()
    total = norm_recv[0]
    for i in range(1, 32):
        total = total + norm_recv[i]
    norm_out[...] = total * FACTOR
    for d in range(1, 16):
        other, copy = part_copy(d)
        pl.when(other < PARTS)(copy.wait_send)

    @pl.when(owner)
    def _():
        for d in range(1, 32):
            sum_copy(d)[1].wait_send()

    for d in range(1, 32):
        other = lax.rem(me + d, 32)
        other_chip = other // 2
        copy = remote(
            part_sum,
            param_out.at[other % 2, pl.ds(lax.rem(other_chip, PARTS) * PART, PART)],
            g_ssem.at[d],
            g_rsem.at[other],
            other,
        )
        pl.when(other_chip < PARTS)(copy.wait_recv)
    for n in range(4):
        drain(n)
    for copy in stores:
        copy.wait()


def shards(
    fields, cotangent, norm_gain, norm_shift, first_weight, first_bias, second_weight, second_bias
):
    def rows(values):
        return values.reshape(8, 3, PAIRS, 128).transpose(1, 2, 0, 3).reshape(3, REAL, 128)

    def unrows(values):
        return values.reshape(3, PAIRS, 8, 128).transpose(2, 0, 1, 3).reshape(1, 8, 3, LON * 64)

    norm = jnp.concatenate([norm_gain.reshape(3, 64), norm_shift.reshape(3, 64)])
    norm = jnp.pad(jnp.concatenate([norm, norm], axis=1), ((0, 2), (0, 0)))
    square = (2, 2, BLOCK, BLOCK)
    weights = jnp.stack([first_weight.reshape(square), second_weight.reshape(square)])
    biases = jnp.stack([first_bias, second_bias])[:, :, :, None, :]
    weights = jnp.concatenate([weights, biases], axis=3)
    weights = jnp.pad(weights, ((0, 0),) * 3 + ((0, 128 - BLOCK - 1), (0, 128 - BLOCK)))
    tables = make_tables()
    buffer = pltpu.VMEM((32, CHUNK, 128), F32)
    middle = pltpu.VMEM((18, CHUNK, 128), F32)
    strips = pltpu.VMEM((3 * STRIP, 128), F32)
    dma = pltpu.SemaphoreType.DMA
    vmem = pl.BlockSpec(memory_space=pltpu.VMEM)
    anywhere = pl.BlockSpec(memory_space=pl.ANY)
    mixed, grad, params, norms = pl.pallas_call(
        kernel,
        out_shape=(
            jax.ShapeDtypeStruct((3, REAL, 128), F32),
            jax.ShapeDtypeStruct((3, REAL, 128), F32),
            jax.ShapeDtypeStruct((2, 4 * GRAD_ROWS, 128), F32),
            jax.ShapeDtypeStruct((8, 128), F32),
        ),
        in_specs=[anywhere] * 2 + [vmem] * 11,
        out_specs=[anywhere] * 2 + [vmem] * 2,
        scratch_shapes=[
            strips,
            strips,
            pltpu.VMEM((STRIP, 128), F32),
            strips,
        ]
        + [buffer] * 8
        + [middle] * 4
        + [
            buffer,
            buffer,
            pltpu.VMEM((4, 3, 256, 256), BF16),
            pltpu.VMEM((4, 256, 256), F32),
            pltpu.VMEM((4, 8, 256), F32),
            pltpu.VMEM((4, 8, 256), F32),
            pltpu.VMEM((2, 8, STRIP), F32),
            pltpu.VMEM((2, 4, 8, STRIP), F32),
            pltpu.VMEM((4 * GRAD_ROWS, 128), F32),
            pltpu.VMEM((16, PART, 128), F32),
            pltpu.VMEM((PART, 128), F32),
            pltpu.VMEM((8, 128), F32),
            pltpu.VMEM((32, 8, 128), F32),
            dma((6,)),
            dma((2, 4)),
            dma((2, 4)),
            dma((4, 49)),
            dma((4, 32)),
            dma((4, 18)),
            dma((16,)),
            dma((16,)),
            dma((32,)),
            dma((32,)),
            dma((32,)),
            dma((32,)),
        ],
        compiler_params=pltpu.CompilerParams(
            collective_id=1, has_side_effects=True, vmem_limit_bytes=63 * 2**20
        ),
        cost_estimate=pl.CostEstimate(
            flops=5_500_000_000, bytes_accessed=12_000_000, transcendentals=0
        ),
        name="mixer",
    )(rows(fields), rows(cotangent), norm, weights, *tables)
    params = params.reshape(2, 2, 2, GRAD_ROWS, 128)[..., :BLOCK].transpose(1, 2, 0, 3, 4)
    flat = (2, 2, BLOCK * BLOCK)
    return (
        unrows(mixed),
        unrows(grad),
        norms[0:3, :64].reshape(LOCAL),
        norms[3:6, :64].reshape(LOCAL),
        params[0, :, :, :BLOCK].reshape(flat),
        params[0, :, :, BLOCK],
        params[1, :, :, :BLOCK].reshape(flat),
        params[1, :, :, BLOCK],
    )


def solution(mesh):
    big = P(None, "lat", "chan", None)
    small = P(None, "chan", None)
    return jax.shard_map(
        shards,
        mesh=mesh,
        in_specs=(big, big, P("chan"), P("chan"), small, small, small, small),
        out_specs=(big, big, P("chan"), P("chan"), small, small, small, small),
        check_vma=False,
    )
```

```python
import functools
import math

import jax
import jax.numpy as jnp
import ml_dtypes
import numpy as np
from jax import lax
from jax.experimental import pallas as pl
from jax.experimental.pallas import tpu as pltpu
from jax.sharding import PartitionSpec as P

F32 = jnp.float32
BF16 = jnp.bfloat16
MESH = pl.DeviceIdType.MESH

LON = 450
EMBED = 768
LOCAL = 192
BLOCK = 96
PAIRS = 225
PADDED = 240
STRIP = PADDED * 8
REAL = PAIRS * 8
RANK = 112
TALL = 120
OWN = 7
KINDS = 3
CHUNK = OWN * KINDS * 8
PIECE = 384
WIDE = 4 * BLOCK
QUARTER = BLOCK // 4
GRAD_ROWS = 4 * QUARTER + 8
PART = 8
PARTS = GRAD_ROWS // PART
EARLY = 4

epsilon = 1e-05
shrink_level = 0.05

SIX = ((1, 1), (0, 2), (2, 0), (0, 1), (1, 0), (0, 0))
THREE = ((0, 1), (1, 0), (0, 0))
FACTOR = 1.0 / math.sqrt(256 * LON)


def split_table(values, count):
    parts = []
    rest = values.astype(np.float64)
    for _ in range(count):
        part = rest.astype(np.float32).astype(ml_dtypes.bfloat16)
        parts.append(part)
        rest = rest - part.astype(np.float64)
    return np.stack(parts)


def make_tables():
    order = np.array([0] + list(range(2, 113)) + [1])
    places = np.arange(PAIRS)
    angles = 2.0 * np.pi * (order[:, None] * places[None, :] % PAIRS) / PAIRS
    plain = np.zeros((PADDED, PADDED))
    plain[: len(order), :PAIRS] = np.cos(angles) / np.sqrt(LON)
    plain[TALL : TALL + len(order), :PAIRS] = -np.sin(angles) / np.sqrt(LON)
    scale = np.full(TALL, 2.0)
    scale[0] = 1.0
    double = plain * np.concatenate([scale, scale])[:, None]
    turn = np.zeros((2, TALL, 128), np.float32)
    turn[0, :, :64] = 1.0
    turn[0, : len(order), 64:] = np.cos(2.0 * np.pi * order / LON)[:, None]
    turn[1, : len(order), 64:] = np.sin(2.0 * np.pi * order / LON)[:, None]
    rows = np.arange(256)
    lat_angles = 2.0 * np.pi * (rows[:, None] * rows[None, :] % 256) / 256
    lat = np.concatenate([np.cos(lat_angles), np.sin(lat_angles)]) / 16.0
    place = np.zeros((2, 2, 2, 128, 256), np.float32)
    for core in range(2):
        for mode in range(2):
            for part in range(2):
                for i in range(BLOCK):
                    in_shared = i >= 64 if core == 0 else i < 32
                    if in_shared:
                        lane = 128 + 64 * part + 32 * mode + i % 32
                    else:
                        lane = 64 * part + (i if core == 0 else i - 32)
                    place[core, mode, part, i, lane] = 1.0
    ones = np.kron(np.eye(2), np.ones((64, 64)))
    bf = ml_dtypes.bfloat16
    return (
        split_table(plain, 3),
        split_table(double, 2),
        split_table(plain.T, 2),
        split_table(double.T, 2),
        split_table(lat, 3),
        turn,
        place.astype(bf),
        np.swapaxes(place, -1, -2).astype(bf),
        ones.astype(bf),
    )


def split(value, count):
    parts = []
    for _ in range(count):
        part = value.astype(BF16)
        parts.append(part)
        value = value - part.astype(F32)
    return parts


def dots(left, right, pairs, dims=((1,), (0,))):
    total = None
    for i, j in pairs:
        term = lax.dot_general(left[i], right[j], (dims, ((), ())), preferred_element_type=F32)
        total = term if total is None else total + term
    return total


def kernel(
    fields,
    cotangent,
    gain,
    shift,
    weight1,
    bias1,
    weight2,
    bias2,
    plain_in,
    double_in,
    back_plain_in,
    back_double_in,
    lat_in,
    turn_in,
    place_in,
    place_t_in,
    ones,
    mixed_out,
    grad_out,
    param_out,
    norm_out,
    plain,
    double,
    back_plain,
    back_double,
    lat_table,
    turn,
    place,
    place_t,
    scaled,
    cot,
    inv,
    result,
    send1,
    send2,
    send3,
    send4,
    recv1,
    recv2,
    recv3,
    recv4,
    mid1,
    mid2,
    mid3,
    mid4,
    act,
    shrunk,
    mats,
    mats_grad,
    sums_grad,
    bias,
    norm,
    weights,
    stage,
    zsend,
    zrecv,
    part_send,
    part_recv,
    part_sum,
    param_all,
    norm_send,
    norm_recv,
    io_sem,
    table_sem,
    z_ssem,
    z_rsem,
    s_sem,
    r_sem,
    m_sem,
    p_ssem,
    p_rsem,
    g_ssem,
    g_rsem,
    c_sem,
    n_ssem,
    n_rsem,
):
    me = lax.axis_index("lat")
    zed = lax.axis_index("chan")
    y, x, core = me // 8, (me // 2) % 4, me % 2
    chip = y * 4 + x
    lane = lax.broadcasted_iota(jnp.int32, (1, 128), 1)
    low = lane < 64
    low32 = lane % 64 < 32
    sign = jnp.where(low, 1.0, -1.0).astype(F32)

    sends = (send1, send2, send3, send4, send4, send3)
    recvs = (recv1, recv2, recv3, recv4, recv4, recv3)
    mids = (mid1, mid2, mid3, mid4, mid4, mid3)
    spans = ((0, OWN), (0, OWN), (0, EARLY), (0, EARLY), (EARLY, OWN), (EARLY, OWN))

    def at(dy, dx):
        return lax.rem(y + dy, 4), lax.rem(x + dx, 4)

    def index(row, column, half):
        return (row * 4 + column) * 2 + half

    def row_slot(row, column, half):
        return half * 16 + row * 4 + column

    def slots(n):
        return (row_slot, index) if n < 2 else (index, row_slot)

    direct = [(0, 0, 2)] + [(0, d, k) for d in (1, 3, 2) for k in (0, 1)]
    direct += [(d, 0, k) for d in (1, 3, 2) for k in (0, 1)]
    latin = [(1, 1), (3, 3), (2, 2), (1, 3), (3, 2), (2, 1), (1, 2), (3, 1), (2, 3)]
    corner = [(dy, dx, k) for dy, dx in latin for k in (0, 1)]

    def corner_slot(dy, dx, k):
        return k * 9 + (dy - 1) * 3 + dx - 1

    def remote(src, dst, ssem, rsem, device):
        return pltpu.make_async_remote_copy(
            src_ref=src,
            dst_ref=dst,
            send_sem=ssem,
            recv_sem=rsem,
            device_id=(device, zed),
            device_id_type=MESH,
        )

    def chunk(n, ref, slot):
        first, last = spans[n]
        return ref.at[slot, pl.ds(24 * first, 24 * (last - first))]

    def first_leg(n, i):
        dy, dx, k = corner[i]
        row, column = at(dy, dx)
        src_slot = slots(n)[0](row, column, k)
        slot = corner_slot(dy, dx, k)
        device = index(y, column, core) if k == 0 else index(row, x, core)
        return remote(
            chunk(n, sends[n], src_slot),
            chunk(n, mids[n], slot),
            s_sem.at[n, i],
            m_sem.at[n, slot],
            device,
        )

    def second_leg(n, i):
        dy, dx, k = corner[i]
        slot = corner_slot(dy, dx, k)
        if k == 0:
            origin = (y, lax.rem(x + 4 - dx, 4))
            final = (lax.rem(y + dy, 4), x)
        else:
            origin = (lax.rem(y + 4 - dy, 4), x)
            final = (y, lax.rem(x + dx, 4))
        return remote(
            chunk(n, mids[n], slot),
            chunk(n, recvs[n], slots(n)[1](origin[0], origin[1], core)),
            s_sem.at[n, 18 + i],
            r_sem.at[n, index(origin[0], origin[1], core)],
            index(final[0], final[1], k),
        )

    def direct_leg(n, i):
        dy, dx, k = direct[i]
        half = 1 - core if k == 2 else k
        row, column = at(dy, dx)
        return remote(
            chunk(n, sends[n], slots(n)[0](row, column, half)),
            chunk(n, recvs[n], slots(n)[1](y, x, core)),
            s_sem.at[n, 36 + i],
            r_sem.at[n, me],
            index(row, column, half),
        )

    def start(n, halves=(0, 1)):
        for i in range(18):
            if corner[i][2] in halves:
                first_leg(n, i).start()
        for i in range(1, 13):
            if direct[i][2] in halves:
                direct_leg(n, i).start()
        if 1 in halves:
            direct_leg(n, 0).start()
            mine = slots(n)[0](y, x, core)
            theirs = slots(n)[1](y, x, core)
            here = pl.ds(24 * spans[n][0], 24 * (spans[n][1] - spans[n][0]))
            recvs[n][theirs, here] = sends[n][mine, here]

    def forward(n, first=0, last=18):
        for i in range(first, last):
            first_leg(n, i).wait_recv()
            second_leg(n, i).start()

    def finish(n):
        for d in range(1, 32):
            origin = lax.rem(me + d, 32)
            slot = slots(n)[1](origin // 8, (origin // 2) % 4, origin % 2)
            remote(
                chunk(n, sends[n], 0), chunk(n, recvs[n], slot), s_sem.at[n, 0], r_sem.at[n, origin], origin
            ).wait_recv()

    def drain(n):
        for i in range(18):
            first_leg(n, i).wait_send()
            second_leg(n, i).wait_send()
        for i in range(13):
            direct_leg(n, i).wait_send()

    def exchange(stage):
        copies = []
        for d in range(1, 4):
            other = lax.rem(zed + d, 4)
            copies.append(
                pltpu.make_async_remote_copy(
                    src_ref=zsend.at[stage],
                    dst_ref=zrecv.at[stage, zed],
                    send_sem=z_ssem.at[stage, d],
                    recv_sem=z_rsem.at[stage, zed],
                    device_id=(me, other),
                    device_id_type=MESH,
                )
            )
        for copy in copies:
            copy.start()
        zrecv[stage, zed] = zsend[stage]
        return copies

    def exchange_wait(stage, copies):
        for copy in copies:
            copy.wait_send()
        for d in range(1, 4):
            other = lax.rem(zed + d, 4)
            pltpu.make_async_remote_copy(
                src_ref=zsend.at[stage],
                dst_ref=zrecv.at[stage, other],
                send_sem=z_ssem.at[stage, d],
                recv_sem=z_rsem.at[stage, other],
                device_id=(me, other),
                device_id_type=MESH,
            ).wait_recv()

    lane48 = lax.broadcasted_iota(jnp.int32, (48, 8, 128), 2) % 64
    own_lane = lane48 == lax.broadcasted_iota(jnp.int32, (48, 8, 128), 0)

    def token_sums(value):
        total = None
        for part in reversed(split(value, 3)):
            term = jnp.dot(part, ones[...], preferred_element_type=F32)
            total = term if total is None else total + term
        return total

    def pack(value):
        return jnp.sum(jnp.where(own_lane, value.reshape(48, 8, 128), 0.0), axis=0)

    def spread(rows):
        return token_sums(jnp.where(own_lane, rows[None], 0.0).reshape(PIECE, 128))

    def lon_forward(load, table, pairs, out, groups):
        count = 3 if pairs is SIX else 2
        flat = out.reshape(32 * CHUNK, 128)
        cos_turn, sin_turn = turn[0], turn[1]
        top = lax.broadcasted_iota(jnp.int32, (TALL, 128), 0) == 0
        for g in groups:

            def body(step, carry, g=g):
                h0 = step * 2
                data = jnp.concatenate([load(g, h0), load(g, h0 + 1)], axis=1)
                parts = split(data, count)
                both = dots([table[i] for i in range(count)], parts, pairs)
                for e in range(2):
                    real = both[:TALL, 128 * e : 128 * e + 128]
                    imag = both[TALL:, 128 * e : 128 * e + 128]
                    turned_real = real * cos_turn + imag * sin_turn
                    turned_imag = imag * cos_turn - real * sin_turn
                    even = jnp.where(low, turned_real, pltpu.roll(turned_imag, 64, 1))
                    odd = jnp.where(low, pltpu.roll(turned_real, 64, 1), turned_imag)
                    a = even + odd
                    b = (even - odd) * sign
                    b = jnp.where(top, a[RANK : RANK + 1], b)
                    h = h0 + e

                    def store(half, kind, value):
                        flat[pl.ds(half * 16 * CHUNK + kind * 8 + h, RANK, stride=24), :] = value[
                            :RANK
                        ]

                    if g == 1:
                        store(0, 2, jnp.where(low32, a, pltpu.roll(b, 32, 1)))
                        store(1, 2, jnp.where(low32, pltpu.roll(a, 96, 1), b))
                    else:
                        store(g // 2, 0, a)
                        store(g // 2, 1, b)
                return carry

            lax.fori_loop(0, 4, body, 0)

    def lon_inverse(source, table, groups):
        flat = source.reshape(32 * CHUNK, 128)
        cos_turn, sin_turn = turn[0], turn[1]
        top = lax.broadcasted_iota(jnp.int32, (RANK, 128), 0) == 0
        top8 = lax.broadcasted_iota(jnp.int32, (8, 128), 0) == 0
        for g in groups:

            def body(step, carry, g=g):
                h0 = step * 2
                columns = []
                for e in range(2):
                    h = h0 + e

                    def fetch(half, kind):
                        return flat[pl.ds(half * 16 * CHUNK + kind * 8 + h, RANK, stride=24), :]

                    if g == 1:
                        u0, u1 = fetch(0, 2), fetch(1, 2)
                        a = jnp.where(low32, u0, pltpu.roll(u1, 32, 1))
                        b = jnp.where(low32, pltpu.roll(u0, 96, 1), u1)
                    else:
                        a, b = fetch(g // 2, 0), fetch(g // 2, 1)
                    last = jnp.where(top8, b[0:1], 0.0)
                    b = jnp.where(top, 0.0, b * sign)
                    even = jnp.concatenate([a + b, last], axis=0)
                    odd = jnp.concatenate([a - b, last], axis=0)
                    real = jnp.where(low, even, pltpu.roll(odd, 64, 1))
                    imag = jnp.where(low, pltpu.roll(even, 64, 1), odd)
                    turned_real = real * cos_turn - imag * sin_turn
                    turned_imag = imag * cos_turn + real * sin_turn
                    columns.append(jnp.concatenate([turned_real, turned_imag], axis=0))
                data = jnp.concatenate(columns, axis=1)
                out = dots([table[0], table[1]], split(data, 2), THREE)
                for e in range(2):
                    result[pl.ds(g * STRIP + h0 + e, PADDED, stride=8), :] = out[
                        :, 128 * e : 128 * e + 128
                    ]
                return carry

            lax.fori_loop(0, 4, body, 0)

    def piece(ref, r, kind):
        return ref[:, pl.ds(pl.multiple_of(r * 24 + kind * 8, 8), 8), :].reshape(256, 128)

    def put(ref, r, kind, value):
        ref[:, pl.ds(pl.multiple_of(r * 24 + kind * 8, 8), 8), :] = value.reshape(32, 8, 128)

    def lat_mix(pieces, orient, pairs):
        count = 3 if pairs is SIX else 2
        data = jnp.concatenate(pieces, axis=1)
        both = dots([lat_table[i] for i in range(count)], split(data, count), pairs)
        out = []
        for kind in range(3):
            direct_part = both[:256, 128 * kind : 128 * kind + 128]
            turned = both[256:, 128 * kind : 128 * kind + 128]
            out.append(direct_part + (orient * sign) * pltpu.roll(turned, 64, 1))
        return out

    def apply(pieces, layer, pairs, transposed):
        count = 3 if pairs is SIX else 2
        dims = ((1,), (1,)) if transposed else ((1,), (0,))
        parts = [split(value, count) for value in pieces]
        out = []
        for mode in range(2):
            left = [
                jnp.concatenate([parts[mode][i], parts[2][i]], axis=1) for i in range(count)
            ]
            right = [mats[layer * 2 + mode, i] for i in range(count)]
            out.append(dots(left, right, pairs, dims))
        return [out[0][:, :128], out[1][:, :128], out[0][:, 128:] + out[1][:, 128:]]

    def mat_grad(inputs, outputs, layer):
        left = [split(value, 2) for value in inputs]
        right = [split(value, 2) for value in outputs]
        for mode in range(2):
            lhs = [jnp.concatenate([left[mode][i], left[2][i]], axis=1) for i in range(2)]
            rhs = [jnp.concatenate([right[mode][i], right[2][i]], axis=1) for i in range(2)]
            mats_grad[layer * 2 + mode] += dots(lhs, rhs, THREE, ((0,), (0,)))
            total = jnp.concatenate([outputs[mode], outputs[2]], axis=1)
            sums_grad[layer * 2 + mode] += jnp.sum(total.reshape(32, 8, 256), axis=0)

    loads = []
    for i, (source, target) in enumerate(((fields, scaled), (cotangent, cot))):
        for g in range(3):
            loads.append(
                pltpu.make_async_copy(
                    source.at[g], target.at[pl.ds(g * STRIP, REAL)], io_sem.at[3 * i + g]
                )
            )
    pairs = (
        (turn_in, turn),
        (double_in, double),
        (plain_in, plain),
        (place_in, place),
        (place_t_in, place_t),
        (lat_in, lat_table),
        (back_plain_in, back_plain),
        (back_double_in, back_double),
    )
    tables = [
        pltpu.make_async_copy(source, target, table_sem.at[i])
        for i, (source, target) in enumerate(pairs)
    ]
    for copy in loads[:3]:
        copy.start()
    barrier = pltpu.get_barrier_semaphore()
    for d in range(1, 32):
        pl.semaphore_signal(
            barrier, inc=1, device_id=(lax.rem(me + d, 32), zed), device_id_type=MESH
        )
    for d in range(1, 4):
        pl.semaphore_signal(
            barrier, inc=1, device_id=(me, lax.rem(zed + d, 4)), device_id_type=MESH
        )
    for g in range(3):
        cot[pl.ds(g * STRIP + REAL, STRIP - REAL), :] = jnp.zeros((STRIP - REAL, 128), F32)
        scaled[pl.ds(g * STRIP + REAL, STRIP - REAL), :] = jnp.zeros((STRIP - REAL, 128), F32)
    for i, source in enumerate((gain, shift)):
        for g in range(3):
            value = source[:, 64 * g : 64 * g + 64]
            norm[3 * i + g : 3 * i + g + 1, :] = jnp.concatenate([value, value], axis=1)
    for copy in loads[:3]:
        copy.wait()
    for copy in tables[:2] + loads[3:] + tables[2:]:
        copy.start()

    def stats_body(k, carry):
        first = pl.multiple_of(k * PIECE, PIECE)
        rows = [scaled[pl.ds(g * STRIP + first, PIECE), :] for g in range(3)]
        here = token_sums(rows[0] + rows[1] + rows[2])
        mean = here * (1.0 / LOCAL)
        square = None
        for value in rows:
            centred = value - mean
            square = centred * centred if square is None else square + centred * centred
        zsend[0, 0, k] = pack(here)
        zsend[0, 1, k] = pack(token_sums(square))
        return carry

    lax.fori_loop(0, STRIP // PIECE, stats_body, 0)
    pl.semaphore_wait(barrier, 34)
    copies = exchange(0)

    def load_cot(g, h):
        return cot[pl.ds(g * STRIP + h, PADDED, stride=8), :]

    for copy in loads[3:] + tables[:2]:
        copy.wait()
    lon_forward(load_cot, double, THREE, send2, (0,))
    exchange_wait(0, copies)

    def norm_body(k, carry):
        sums = [zrecv[0, i, 0, k] for i in range(4)]
        squares = [zrecv[0, i, 1, k] for i in range(4)]
        mean = ((sums[0] + sums[1]) + (sums[2] + sums[3])) * (1.0 / EMBED)
        apart = None
        for value in sums:
            gap = value * (1.0 / LOCAL) - mean
            apart = gap * gap if apart is None else apart + gap * gap
        total = (squares[0] + squares[1]) + (squares[2] + squares[3]) + apart * LOCAL
        inverse = spread(lax.rsqrt(total * (1.0 / EMBED) + epsilon))
        mean = spread(mean)
        first = pl.multiple_of(k * PIECE, PIECE)
        inv[pl.ds(first, PIECE), :] = inverse
        for g in range(3):
            here = pl.ds(g * STRIP + first, PIECE)
            scaled[here, :] = (scaled[here, :] - mean) * inverse
        return carry

    lax.fori_loop(0, STRIP // PIECE, norm_body, 0)

    def load_normed(g, h):
        value = scaled[pl.ds(g * STRIP + h, PADDED, stride=8), :]
        return value * norm[g : g + 1] + norm[3 + g : 4 + g]

    tables[2].wait()
    lon_forward(load_normed, plain, SIX, send1, (0, 1))
    start(0, (0,))
    lon_forward(load_normed, plain, SIX, send1, (2,))
    start(0, (1,))
    lon_forward(load_cot, double, THREE, send2, (1, 2))

    for copy in tables[3:]:
        copy.wait()
    for layer, (weight, shifts) in enumerate(((weight1, bias1), (weight2, bias2))):
        for part in range(2):
            target = weights.at[layer * 2 + part]
            target[...] = jnp.zeros((128, 128), F32)
            for q in range(24):
                stage[q : q + 1, :] = weight[part, pl.ds(core, 1), 384 * q : 384 * q + 384]
            for t in range(4):
                value = stage[:, BLOCK * t : BLOCK * t + BLOCK]
                value = jnp.concatenate([value, jnp.zeros((24, 128 - BLOCK), F32)], axis=1)
                target[pl.ds(t, 24, stride=4), :] = value
            value = shifts[part, pl.ds(core, 1), :]
            target[BLOCK : BLOCK + 1, :BLOCK] = value
    for layer in range(2):
        for mode in range(2):
            to_real, to_imag = place[core, mode, 0], place[core, mode, 1]
            real = split(weights[layer * 2], 3)
            imag = split(weights[layer * 2 + 1], 3)

            def fan(parts, target):
                total = None
                for part in reversed(parts):
                    term = jnp.dot(part, target, preferred_element_type=F32)
                    total = term if total is None else total + term
                return total

            upper = fan(real, to_real) + fan(imag, to_imag)
            lower = fan(real, to_imag) - fan(imag, to_real)
            bias[layer * 2 + mode] = jnp.broadcast_to(upper[BLOCK : BLOCK + 1], (8, 256))

            def lift(source, value):
                total = None
                for part in reversed(split(value, 3)):
                    term = jnp.dot(source, part, preferred_element_type=F32)
                    total = term if total is None else total + term
                return total

            whole = lift(place_t[core, mode, 0], upper) + lift(place_t[core, mode, 1], lower)
            for i, part in enumerate(split(whole, 3)):
                mats[layer * 2 + mode, i] = part
    forward(0)
    start(1)

    def add_bias(pieces, layer):
        first, second = bias[layer * 2], bias[layer * 2 + 1]
        return [
            pieces[0] + first[0:1, :128],
            pieces[1] + second[0:1, :128],
            pieces[2] + (first[0:1, 128:] + second[0:1, 128:]),
        ]

    finish(0)

    def forward_body(r, carry):
        spectrum = lat_mix([piece(recv1, r, kind) for kind in range(3)], 1.0, SIX)
        for kind in range(3):
            put(recv1, r, kind, spectrum[kind])
        hidden = [jnp.maximum(v, 0.0) for v in add_bias(apply(spectrum, 0, SIX, False), 0)]
        for kind in range(3):
            put(act, r, kind, hidden[kind])
        out = add_bias(apply(hidden, 1, SIX, False), 1)
        out = [v - jnp.clip(v, -shrink_level, shrink_level) for v in out]
        for kind in range(3):
            put(shrunk, r, kind, out[kind])
        rows = lat_mix(out, -1.0, THREE)
        for kind in range(3):
            put(send3, r, kind, rows[kind])
        return carry

    forward(1)
    lax.fori_loop(0, EARLY, forward_body, 0)
    start(2)
    lax.fori_loop(EARLY, OWN, forward_body, 0)
    finish(1)

    mats_grad[...] = jnp.zeros_like(mats_grad)
    sums_grad[...] = jnp.zeros_like(sums_grad)

    def backward_body(r, carry):
        upstream = lat_mix([piece(recv2, r, kind) for kind in range(3)], 1.0, THREE)
        out_grad = [
            jnp.where(piece(shrunk, r, kind) != 0.0, upstream[kind], 0.0) for kind in range(3)
        ]
        hidden = [piece(act, r, kind) for kind in range(3)]
        mat_grad(hidden, out_grad, 1)
        hidden_grad = apply(out_grad, 1, THREE, True)
        pre_grad = [jnp.where(h > 0.0, g, 0.0) for h, g in zip(hidden, hidden_grad)]
        mat_grad([piece(recv1, r, kind) for kind in range(3)], pre_grad, 0)
        rows = lat_mix(apply(pre_grad, 0, THREE, True), -1.0, THREE)
        for kind in range(3):
            put(send4, r, kind, rows[kind])
        return carry

    lax.fori_loop(0, 2, backward_body, 0)
    forward(2)
    lax.fori_loop(2, EARLY, backward_body, 0)
    start(3)
    lax.fori_loop(EARLY, OWN, backward_body, 0)

    bias_row = lax.broadcasted_iota(jnp.int32, (128, 128), 0) == BLOCK
    for layer in range(2):
        real_total, imag_total = None, None
        for mode in range(2):
            real_t, imag_t = place_t[core, mode, 0], place_t[core, mode, 1]
            real_p, imag_p = place[core, mode, 0], place[core, mode, 1]
            grads = split(mats_grad[layer * 2 + mode], 2)
            to_real = sum(jnp.dot(v, real_t, preferred_element_type=F32) for v in grads)
            to_imag = sum(jnp.dot(v, imag_t, preferred_element_type=F32) for v in grads)

            def lower_to(target, value):
                return sum(
                    jnp.dot(target, v, preferred_element_type=F32) for v in split(value, 2)
                )

            real = lower_to(real_p, to_real) + lower_to(imag_p, to_imag)
            imag = lower_to(real_p, to_imag) - lower_to(imag_p, to_real)
            column = jnp.sum(sums_grad[layer * 2 + mode], axis=0, keepdims=True)
            column = jnp.broadcast_to(column, (16, 256))
            sums = split(column, 3)
            real_bias = sum(jnp.dot(v, real_t, preferred_element_type=F32) for v in sums)
            imag_bias = sum(jnp.dot(v, imag_t, preferred_element_type=F32) for v in sums)
            real = jnp.where(bias_row, real_bias[0:1], real)
            imag = jnp.where(bias_row, imag_bias[0:1], imag)
            real_total = real if real_total is None else real_total + real
            imag_total = imag if imag_total is None else imag_total + imag
        for part, value in enumerate((real_total, imag_total)):
            weights[layer * 2 + part] = value
    for i in range(4):
        columns = [
            weights[i, pl.ds(t, QUARTER, stride=4), :][:, :BLOCK] for t in range(4)
        ]
        part_send[pl.ds(i * QUARTER, QUARTER), :] = jnp.concatenate(columns, axis=1)
    row = jnp.concatenate([weights[i, BLOCK : BLOCK + 1, :][:, :BLOCK] for i in range(4)], axis=1)
    top = lax.broadcasted_iota(jnp.int32, (8, WIDE), 0) == 0
    part_send[pl.ds(4 * QUARTER, 8), :] = jnp.where(top, row, 0.0)

    def part_copy(d):
        other = lax.rem(chip + d, 16)
        return other, remote(
            part_send.at[pl.ds(lax.rem(other, PARTS) * PART, PART)],
            part_recv.at[chip],
            p_ssem.at[d],
            p_rsem.at[chip],
            other * 2 + core,
        )

    for d in range(1, 16):
        other, copy = part_copy(d)
        pl.when(other < PARTS)(copy.start)
    part_recv[chip] = part_send[pl.ds(lax.rem(chip, PARTS) * PART, PART), :]
    forward(3)
    start(4)

    owner = chip < PARTS

    def sum_copy(d):
        other = lax.rem(chip + d, 16)
        return remote(
            part_sum,
            param_all.at[core, pl.ds(lax.rem(chip, PARTS) * PART, PART)],
            g_ssem.at[d],
            g_rsem.at[chip],
            other * 2 + core,
        )

    @pl.when(owner)
    def _():
        for d in range(1, 16):
            other = lax.rem(chip + d, 16)
            remote(
                part_send.at[pl.ds(0, PART)],
                part_recv.at[other],
                p_ssem.at[d],
                p_rsem.at[other],
                other * 2 + core,
            ).wait_recv()
        total = part_recv[0]
        for i in range(1, 16):
            total = total + part_recv[i]
        part_sum[...] = total * FACTOR
        param_all[core, pl.ds(lax.rem(chip, PARTS) * PART, PART), :] = total * FACTOR
        for d in range(1, 16):
            sum_copy(d).start()

    forward(4)
    start(5)

    for d in range(1, 16):
        other = lax.rem(chip + d, 16)
        copy = remote(
            part_sum,
            param_all.at[core, pl.ds(lax.rem(other, PARTS) * PART, PART)],
            g_ssem.at[d],
            g_rsem.at[other],
            other * 2 + core,
        )
        pl.when(other < PARTS)(copy.wait_recv)
    across = remote(
        param_all.at[core], param_all.at[core], c_sem.at[0], c_sem.at[1], index(y, x, 1 - core)
    )
    across.start()
    finish(3)
    finish(4)

    lon_inverse(recv4, back_plain, (0, 1, 2))

    def sums_body(k, gains):
        direct_sum, cross_sum = None, None
        gains = list(gains)
        first = pl.multiple_of(k * PIECE, PIECE)
        for g in range(3):
            here = pl.ds(g * STRIP + first, PIECE)
            normed_grad = cot[here, :] + result[here, :]
            unit = scaled[here, :]
            for slot, value in ((g, normed_grad * unit), (3 + g, normed_grad)):
                gains[slot] += jnp.sum(value.reshape(PIECE // 8, 8, 128), axis=0)
            scaled_grad = normed_grad * norm[g : g + 1]
            cot[here, :] = scaled_grad
            cross = scaled_grad * unit
            direct_sum = scaled_grad if direct_sum is None else direct_sum + scaled_grad
            cross_sum = cross if cross_sum is None else cross_sum + cross
        zsend[1, 0, k] = pack(token_sums(direct_sum))
        zsend[1, 1, k] = pack(token_sums(cross_sum))
        return tuple(gains)

    zero = jnp.zeros((8, 128), F32)
    gains = lax.fori_loop(0, STRIP // PIECE, sums_body, (zero,) * 6)
    copies = exchange(1)
    norm_rows = lax.broadcasted_iota(jnp.int32, (8, 128), 0)
    packed = jnp.zeros((8, 128), F32)
    for i, value in enumerate(gains):
        value = jnp.sum(value, axis=0, keepdims=True)
        packed = jnp.where(norm_rows == i, value, packed)
    norm_send[...] = packed + pltpu.roll(packed, 64, 1)
    norm_recv[me] = norm_send[...]

    def norm_copy(d):
        other = lax.rem(me + d, 32)
        return remote(norm_send, norm_recv.at[me], n_ssem.at[d], n_rsem.at[me], other)

    for d in range(1, 32):
        norm_copy(d).start()
    forward(5)
    exchange_wait(1, copies)

    def grad_body(k, carry):
        means = []
        for which in range(2):
            group = [zrecv[1, i, which, k] for i in range(4)]
            total = (group[0] + group[1]) + (group[2] + group[3])
            means.append(spread(total * (1.0 / EMBED)))
        first = pl.multiple_of(k * PIECE, PIECE)
        inverse = inv[pl.ds(first, PIECE), :]
        for g in range(3):
            here = pl.ds(g * STRIP + first, PIECE)
            cot[here, :] = inverse * (cot[here, :] - means[0] - scaled[here, :] * means[1])
        return carry

    lax.fori_loop(0, STRIP // PIECE, grad_body, 0)
    stores = []
    for g in range(3):
        stores.append(
            pltpu.make_async_copy(
                cot.at[pl.ds(g * STRIP, REAL)], grad_out.at[g], io_sem.at[3 + g]
            )
        )
        stores[-1].start()

    finish(2)
    finish(5)
    for g in range(3):
        lon_inverse(recv3, back_double, (g,))
        here = pl.ds(g * STRIP, REAL)
        result[here, :] = (
            result[here, :] + scaled[here, :] * norm[g : g + 1] + norm[3 + g : 4 + g]
        )
        stores.append(
            pltpu.make_async_copy(
                result.at[pl.ds(g * STRIP, REAL)], mixed_out.at[g], io_sem.at[g]
            )
        )
        stores[-1].start()

    remote(
        param_all.at[1 - core],
        param_all.at[1 - core],
        c_sem.at[0],
        c_sem.at[1],
        index(y, x, 1 - core),
    ).wait_recv()
    across.wait_send()
    param_out[...] = param_all[...]
    for d in range(1, 32):
        other = lax.rem(me + d, 32)
        remote(
            norm_send, norm_recv.at[other], n_ssem.at[d], n_rsem.at[other], other
        ).wait_recv()
        norm_copy(d).wait_send()
    total = norm_recv[0]
    for i in range(1, 32):
        total = total + norm_recv[i]
    norm_out[...] = total * FACTOR
    for d in range(1, 16):
        other, copy = part_copy(d)
        pl.when(other < PARTS)(copy.wait_send)

    @pl.when(owner)
    def _():
        for d in range(1, 16):
            sum_copy(d).wait_send()

    for n in range(6):
        drain(n)
    for copy in stores:
        copy.wait()


def finisher(
    mixed,
    grad,
    params,
    norms,
    mixed_out,
    grad_out,
    gain_out,
    shift_out,
    weight1_out,
    bias1_out,
    weight2_out,
    bias2_out,
    held,
    sem,
):
    loads, stores = [], []
    for i, (source, target) in enumerate(((mixed, mixed_out), (grad, grad_out))):
        for g in range(3):
            for part in range(3):
                n = 9 * i + 3 * g + part
                here = pl.ds(part * (REAL // 3), REAL // 3)
                there = held.at[3 * i + g, here]
                loads.append(pltpu.make_async_copy(source.at[g, here], there, sem.at[n]))
                stores.append(pltpu.make_async_copy(there, target.at[g, here], sem.at[18 + n]))
                loads[-1].start()
    for load, store in zip(loads, stores):
        load.wait()
        store.start()
    gain_out[...] = jnp.concatenate([norms[g : g + 1, :64] for g in range(3)], axis=1)
    shift_out[...] = jnp.concatenate([norms[3 + g : 4 + g, :64] for g in range(3)], axis=1)
    for layer, (weight, shifts) in enumerate(
        ((weight1_out, bias1_out), (weight2_out, bias2_out))
    ):
        for part in range(2):
            i = layer * 2 + part
            for half in range(2):
                for q in range(QUARTER):
                    row = i * QUARTER + q
                    weight[part, half : half + 1, WIDE * q : WIDE * q + WIDE] = params[
                        half, row : row + 1, :
                    ]
                row = params[half, 4 * QUARTER : 4 * QUARTER + 1, :]
                shifts[part, half : half + 1, :] = row[:, BLOCK * i : BLOCK * i + BLOCK]
    for store in stores:
        store.wait()


def shards(
    fields, cotangent, norm_gain, norm_shift, first_weight, first_bias, second_weight, second_bias
):
    def rows(values):
        return values.reshape(8, 3, PAIRS, 128).transpose(1, 2, 0, 3).reshape(3, REAL, 128)

    def unrows(values):
        return values.reshape(3, PAIRS, 8, 128).transpose(2, 0, 1, 3).reshape(1, 8, 3, LON * 64)

    tables = make_tables()
    buffer = pltpu.VMEM((32, CHUNK, 128), F32)
    middle = pltpu.VMEM((18, CHUNK, 128), F32)
    strips = pltpu.VMEM((3 * STRIP, 128), F32)
    dma = pltpu.SemaphoreType.DMA
    vmem = pl.BlockSpec(memory_space=pltpu.VMEM)
    anywhere = pl.BlockSpec(memory_space=pl.ANY)
    wholes = (
        jax.ShapeDtypeStruct((3, REAL, 128), F32),
        jax.ShapeDtypeStruct((3, REAL, 128), F32),
    )
    middles = pl.pallas_call(
        kernel,
        out_shape=wholes
        + (
            jax.ShapeDtypeStruct((2, GRAD_ROWS, WIDE), F32),
            jax.ShapeDtypeStruct((8, 128), F32),
        ),
        in_specs=[anywhere] * 2 + [vmem] * 6 + [anywhere] * 8 + [vmem],
        out_specs=[anywhere] * 2 + [vmem] * 2,
        scratch_shapes=[pltpu.VMEM(table.shape, table.dtype) for table in tables[:8]]
        + [
            strips,
            strips,
            pltpu.VMEM((STRIP, 128), F32),
            strips,
        ]
        + [buffer] * 8
        + [middle] * 4
        + [
            buffer,
            buffer,
            pltpu.VMEM((4, 3, 256, 256), BF16),
            pltpu.VMEM((4, 256, 256), F32),
            pltpu.VMEM((4, 8, 256), F32),
            pltpu.VMEM((4, 8, 256), F32),
            pltpu.VMEM((8, 128), F32),
            pltpu.VMEM((4, 128, 128), F32),
            pltpu.VMEM((24, 384), F32),
            pltpu.VMEM((2, 2, STRIP // PIECE, 8, 128), F32),
            pltpu.VMEM((2, 4, 2, STRIP // PIECE, 8, 128), F32),
            pltpu.VMEM((GRAD_ROWS, WIDE), F32),
            pltpu.VMEM((16, PART, WIDE), F32),
            pltpu.VMEM((PART, WIDE), F32),
            pltpu.VMEM((2, GRAD_ROWS, WIDE), F32),
            pltpu.VMEM((8, 128), F32),
            pltpu.VMEM((32, 8, 128), F32),
            dma((6,)),
            dma((8,)),
            dma((2, 4)),
            dma((2, 4)),
            dma((6, 49)),
            dma((6, 32)),
            dma((6, 18)),
            dma((16,)),
            dma((16,)),
            dma((16,)),
            dma((16,)),
            dma((2,)),
            dma((32,)),
            dma((32,)),
        ],
        compiler_params=pltpu.CompilerParams(
            collective_id=1, has_side_effects=True, vmem_limit_bytes=63 * 2**20
        ),
        cost_estimate=pl.CostEstimate(
            flops=5_500_000_000, bytes_accessed=12_000_000, transcendentals=0
        ),
        name="mixer",
    )(
        rows(fields),
        rows(cotangent),
        norm_gain.reshape(1, LOCAL),
        norm_shift.reshape(1, LOCAL),
        first_weight,
        first_bias,
        second_weight,
        second_bias,
        *tables,
    )
    mixed, grad, *rest = pl.pallas_call(
        finisher,
        out_shape=wholes
        + (
            jax.ShapeDtypeStruct((1, LOCAL), F32),
            jax.ShapeDtypeStruct((1, LOCAL), F32),
            jax.ShapeDtypeStruct(first_weight.shape, F32),
            jax.ShapeDtypeStruct(first_bias.shape, F32),
            jax.ShapeDtypeStruct(second_weight.shape, F32),
            jax.ShapeDtypeStruct(second_bias.shape, F32),
        ),
        in_specs=[anywhere] * 2 + [vmem] * 2,
        out_specs=[anywhere] * 2 + [vmem] * 6,
        scratch_shapes=[pltpu.VMEM((6, REAL, 128), F32), dma((36,))],
        compiler_params=pltpu.CompilerParams(vmem_limit_bytes=63 * 2**20),
        name="finisher",
    )(*middles)
    return (unrows(mixed), unrows(grad), rest[0].reshape(LOCAL), rest[1].reshape(LOCAL), *rest[2:])


def solution(mesh):
    big = P(None, "lat", "chan", None)
    small = P(None, "chan", None)
    return jax.shard_map(
        shards,
        mesh=mesh,
        in_specs=(big, big, P("chan"), P("chan"), small, small, small, small),
        out_specs=(big, big, P("chan"), P("chan"), small, small, small, small),
        check_vma=False,
    )
```

```python
import functools
import math

import jax
import jax.numpy as jnp
import ml_dtypes
import numpy as np
from jax import lax
from jax.experimental import pallas as pl
from jax.experimental.pallas import tpu as pltpu
from jax.sharding import PartitionSpec as P

F32 = jnp.float32
BF16 = jnp.bfloat16
MESH = pl.DeviceIdType.MESH

LON = 450
EMBED = 768
LOCAL = 192
BLOCK = 96
PAIRS = 225
PADDED = 240
STRIP = PADDED * 8
REAL = PAIRS * 8
RANK = 112
TALL = 120
OWN = 7
KINDS = 3
CHUNK = OWN * KINDS * 8
PIECE = 384
WIDE = 4 * BLOCK
QUARTER = BLOCK // 4
GRAD_ROWS = 4 * QUARTER + 8
PART = 8
PARTS = GRAD_ROWS // PART
EARLY = 4

epsilon = 1e-05
shrink_level = 0.05

SIX = ((1, 1), (0, 2), (2, 0), (0, 1), (1, 0), (0, 0))
THREE = ((0, 1), (1, 0), (0, 0))
FACTOR = 1.0 / math.sqrt(256 * LON)


def split_table(values, count):
    parts = []
    rest = values.astype(np.float64)
    for _ in range(count):
        part = rest.astype(np.float32).astype(ml_dtypes.bfloat16)
        parts.append(part)
        rest = rest - part.astype(np.float64)
    return np.stack(parts)


def make_tables():
    order = np.array([0] + list(range(2, 113)) + [1])
    places = np.arange(PAIRS)
    angles = 2.0 * np.pi * (order[:, None] * places[None, :] % PAIRS) / PAIRS
    plain = np.zeros((PADDED, PADDED))
    plain[: len(order), :PAIRS] = np.cos(angles) / np.sqrt(LON)
    plain[TALL : TALL + len(order), :PAIRS] = -np.sin(angles) / np.sqrt(LON)
    scale = np.full(TALL, 2.0)
    scale[0] = 1.0
    double = plain * np.concatenate([scale, scale])[:, None]
    turn = np.zeros((2, TALL, 128), np.float32)
    turn[0, :, :64] = 1.0
    turn[0, : len(order), 64:] = np.cos(2.0 * np.pi * order / LON)[:, None]
    turn[1, : len(order), 64:] = np.sin(2.0 * np.pi * order / LON)[:, None]
    rows = np.arange(256)
    lat_angles = 2.0 * np.pi * (rows[:, None] * rows[None, :] % 256) / 256
    lat = np.concatenate([np.cos(lat_angles), np.sin(lat_angles)]) / 16.0
    place = np.zeros((2, 2, 2, 128, 256), np.float32)
    for core in range(2):
        for mode in range(2):
            for part in range(2):
                for i in range(BLOCK):
                    in_shared = i >= 64 if core == 0 else i < 32
                    if in_shared:
                        lane = 128 + 64 * part + 32 * mode + i % 32
                    else:
                        lane = 64 * part + (i if core == 0 else i - 32)
                    place[core, mode, part, i, lane] = 1.0
    ones = np.kron(np.eye(2), np.ones((64, 64)))
    bf = ml_dtypes.bfloat16
    return (
        split_table(plain, 3),
        split_table(double, 2),
        split_table(plain.T, 2),
        split_table(double.T, 2),
        split_table(lat, 3),
        turn,
        place.astype(bf),
        np.swapaxes(place, -1, -2).astype(bf),
        ones.astype(bf),
    )


def split(value, count):
    parts = []
    for _ in range(count):
        part = value.astype(BF16)
        parts.append(part)
        value = value - part.astype(F32)
    return parts


def dots(left, right, pairs, dims=((1,), (0,))):
    total = None
    for i, j in pairs:
        term = lax.dot_general(left[i], right[j], (dims, ((), ())), preferred_element_type=F32)
        total = term if total is None else total + term
    return total


def kernel(
    fields,
    cotangent,
    gain,
    shift,
    weight1,
    bias1,
    weight2,
    bias2,
    plain_in,
    double_in,
    back_plain_in,
    back_double_in,
    lat_in,
    turn_in,
    place_in,
    place_t_in,
    ones,
    mixed_out,
    grad_out,
    param_out,
    norm_out,
    plain,
    double,
    back_plain,
    back_double,
    lat_table,
    turn,
    place,
    place_t,
    scaled,
    cot,
    inv,
    result,
    send1,
    send2,
    send3,
    send4,
    recv1,
    recv2,
    recv3,
    recv4,
    mid1,
    mid2,
    mid3,
    mid4,
    act,
    shrunk,
    mats,
    mats_grad,
    sums_grad,
    bias,
    norm,
    weights,
    stage,
    zsend,
    zrecv,
    part_send,
    part_recv,
    part_sum,
    param_all,
    norm_send,
    norm_recv,
    io_sem,
    table_sem,
    z_ssem,
    z_rsem,
    s_sem,
    r_sem,
    m_sem,
    p_ssem,
    p_rsem,
    g_ssem,
    g_rsem,
    c_sem,
    n_ssem,
    n_rsem,
):
    me = lax.axis_index("lat")
    zed = lax.axis_index("chan")
    y, x, core = me // 8, (me // 2) % 4, me % 2
    chip = y * 4 + x
    lane = lax.broadcasted_iota(jnp.int32, (1, 128), 1)
    low = lane < 64
    low32 = lane % 64 < 32
    sign = jnp.where(low, 1.0, -1.0).astype(F32)

    sends = (send1, send2, send3, send4, send4, send3)
    recvs = (recv1, recv2, recv3, recv4, recv4, recv3)
    mids = (mid1, mid2, mid3, mid4, mid4, mid3)
    spans = ((0, OWN), (0, OWN), (0, EARLY), (0, EARLY), (EARLY, OWN), (EARLY, OWN))

    def at(dy, dx):
        return lax.rem(y + dy, 4), lax.rem(x + dx, 4)

    def index(row, column, half):
        return (row * 4 + column) * 2 + half

    def row_slot(row, column, half):
        return half * 16 + row * 4 + column

    def slots(n):
        return (row_slot, index) if n < 2 else (index, row_slot)

    direct = [(0, 0, 2)] + [(0, d, k) for d in (1, 3, 2) for k in (0, 1)]
    direct += [(d, 0, k) for d in (1, 3, 2) for k in (0, 1)]
    latin = [(1, 1), (3, 3), (2, 2), (1, 3), (3, 2), (2, 1), (1, 2), (3, 1), (2, 3)]
    corner = [(dy, dx, k) for dy, dx in latin for k in (0, 1)]

    def corner_slot(dy, dx, k):
        return k * 9 + (dy - 1) * 3 + dx - 1

    def remote(src, dst, ssem, rsem, device):
        return pltpu.make_async_remote_copy(
            src_ref=src,
            dst_ref=dst,
            send_sem=ssem,
            recv_sem=rsem,
            device_id=(device, zed),
            device_id_type=MESH,
        )

    def chunk(n, ref, slot):
        first, last = spans[n]
        return ref.at[slot, pl.ds(24 * first, 24 * (last - first))]

    def first_leg(n, i):
        dy, dx, k = corner[i]
        row, column = at(dy, dx)
        src_slot = slots(n)[0](row, column, k)
        slot = corner_slot(dy, dx, k)
        device = index(y, column, core) if k == 0 else index(row, x, core)
        return remote(
            chunk(n, sends[n], src_slot),
            chunk(n, mids[n], slot),
            s_sem.at[n, i],
            m_sem.at[n, slot],
            device,
        )

    def second_leg(n, i):
        dy, dx, k = corner[i]
        slot = corner_slot(dy, dx, k)
        if k == 0:
            origin = (y, lax.rem(x + 4 - dx, 4))
            final = (lax.rem(y + dy, 4), x)
        else:
            origin = (lax.rem(y + 4 - dy, 4), x)
            final = (y, lax.rem(x + dx, 4))
        return remote(
            chunk(n, mids[n], slot),
            chunk(n, recvs[n], slots(n)[1](origin[0], origin[1], core)),
            s_sem.at[n, 18 + i],
            r_sem.at[n, index(origin[0], origin[1], core)],
            index(final[0], final[1], k),
        )

    def direct_leg(n, i):
        dy, dx, k = direct[i]
        half = 1 - core if k == 2 else k
        row, column = at(dy, dx)
        return remote(
            chunk(n, sends[n], slots(n)[0](row, column, half)),
            chunk(n, recvs[n], slots(n)[1](y, x, core)),
            s_sem.at[n, 36 + i],
            r_sem.at[n, me],
            index(row, column, half),
        )

    def start(n, halves=(0, 1)):
        for i in range(18):
            if corner[i][2] in halves:
                first_leg(n, i).start()
        for i in range(1, 13):
            if direct[i][2] in halves:
                direct_leg(n, i).start()
        if 1 in halves:
            direct_leg(n, 0).start()
            mine = slots(n)[0](y, x, core)
            theirs = slots(n)[1](y, x, core)
            here = pl.ds(24 * spans[n][0], 24 * (spans[n][1] - spans[n][0]))
            recvs[n][theirs, here] = sends[n][mine, here]

    def forward(n, first=0, last=18):
        for i in range(first, last):
            first_leg(n, i).wait_recv()
            second_leg(n, i).start()

    def finish(n):
        for d in range(1, 32):
            origin = lax.rem(me + d, 32)
            slot = slots(n)[1](origin // 8, (origin // 2) % 4, origin % 2)
            remote(
                chunk(n, sends[n], 0), chunk(n, recvs[n], slot), s_sem.at[n, 0], r_sem.at[n, origin], origin
            ).wait_recv()

    def drain(n):
        for i in range(18):
            first_leg(n, i).wait_send()
            second_leg(n, i).wait_send()
        for i in range(13):
            direct_leg(n, i).wait_send()

    def exchange(stage):
        copies = []
        for d in range(1, 4):
            other = lax.rem(zed + d, 4)
            copies.append(
                pltpu.make_async_remote_copy(
                    src_ref=zsend.at[stage],
                    dst_ref=zrecv.at[stage, zed],
                    send_sem=z_ssem.at[stage, d],
                    recv_sem=z_rsem.at[stage, zed],
                    device_id=(me, other),
                    device_id_type=MESH,
                )
            )
        for copy in copies:
            copy.start()
        zrecv[stage, zed] = zsend[stage]
        return copies

    def exchange_wait(stage, copies):
        for copy in copies:
            copy.wait_send()
        for d in range(1, 4):
            other = lax.rem(zed + d, 4)
            pltpu.make_async_remote_copy(
                src_ref=zsend.at[stage],
                dst_ref=zrecv.at[stage, other],
                send_sem=z_ssem.at[stage, d],
                recv_sem=z_rsem.at[stage, other],
                device_id=(me, other),
                device_id_type=MESH,
            ).wait_recv()

    lane48 = lax.broadcasted_iota(jnp.int32, (48, 8, 128), 2) % 64
    own_lane = lane48 == lax.broadcasted_iota(jnp.int32, (48, 8, 128), 0)

    def token_sums(value):
        total = None
        for part in reversed(split(value, 3)):
            term = jnp.dot(part, ones[...], preferred_element_type=F32)
            total = term if total is None else total + term
        return total

    def pack(value):
        return jnp.sum(jnp.where(own_lane, value.reshape(48, 8, 128), 0.0), axis=0)

    def spread(rows):
        return token_sums(jnp.where(own_lane, rows[None], 0.0).reshape(PIECE, 128))

    def lon_forward(load, table, pairs, out, groups):
        count = 3 if pairs is SIX else 2
        flat = out.reshape(32 * CHUNK, 128)
        cos_turn, sin_turn = turn[0], turn[1]
        top = lax.broadcasted_iota(jnp.int32, (TALL, 128), 0) == 0
        for g in groups:

            def body(step, carry, g=g):
                h0 = step * 2
                data = jnp.concatenate([load(g, h0), load(g, h0 + 1)], axis=1)
                parts = split(data, count)
                both = dots([table[i] for i in range(count)], parts, pairs)
                for e in range(2):
                    real = both[:TALL, 128 * e : 128 * e + 128]
                    imag = both[TALL:, 128 * e : 128 * e + 128]
                    turned_real = real * cos_turn + imag * sin_turn
                    turned_imag = imag * cos_turn - real * sin_turn
                    even = jnp.where(low, turned_real, pltpu.roll(turned_imag, 64, 1))
                    odd = jnp.where(low, pltpu.roll(turned_real, 64, 1), turned_imag)
                    a = even + odd
                    b = (even - odd) * sign
                    b = jnp.where(top, a[RANK : RANK + 1], b)
                    h = h0 + e

                    def store(half, kind, value):
                        flat[pl.ds(half * 16 * CHUNK + kind * 8 + h, RANK, stride=24), :] = value[
                            :RANK
                        ]

                    if g == 1:
                        store(0, 2, jnp.where(low32, a, pltpu.roll(b, 32, 1)))
                        store(1, 2, jnp.where(low32, pltpu.roll(a, 96, 1), b))
                    else:
                        store(g // 2, 0, a)
                        store(g // 2, 1, b)
                return carry

            lax.fori_loop(0, 4, body, 0, unroll=True)

    def lon_inverse(source, table, groups):
        flat = source.reshape(32 * CHUNK, 128)
        cos_turn, sin_turn = turn[0], turn[1]
        top = lax.broadcasted_iota(jnp.int32, (RANK, 128), 0) == 0
        top8 = lax.broadcasted_iota(jnp.int32, (8, 128), 0) == 0
        for g in groups:

            def body(step, carry, g=g):
                h0 = step * 2
                columns = []
                for e in range(2):
                    h = h0 + e

                    def fetch(half, kind):
                        return flat[pl.ds(half * 16 * CHUNK + kind * 8 + h, RANK, stride=24), :]

                    if g == 1:
                        u0, u1 = fetch(0, 2), fetch(1, 2)
                        a = jnp.where(low32, u0, pltpu.roll(u1, 32, 1))
                        b = jnp.where(low32, pltpu.roll(u0, 96, 1), u1)
                    else:
                        a, b = fetch(g // 2, 0), fetch(g // 2, 1)
                    last = jnp.where(top8, b[0:1], 0.0)
                    b = jnp.where(top, 0.0, b * sign)
                    even = jnp.concatenate([a + b, last], axis=0)
                    odd = jnp.concatenate([a - b, last], axis=0)
                    real = jnp.where(low, even, pltpu.roll(odd, 64, 1))
                    imag = jnp.where(low, pltpu.roll(even, 64, 1), odd)
                    turned_real = real * cos_turn - imag * sin_turn
                    turned_imag = imag * cos_turn + real * sin_turn
                    columns.append(jnp.concatenate([turned_real, turned_imag], axis=0))
                data = jnp.concatenate(columns, axis=1)
                out = dots([table[0], table[1]], split(data, 2), THREE)
                for e in range(2):
                    result[pl.ds(g * STRIP + h0 + e, PADDED, stride=8), :] = out[
                        :, 128 * e : 128 * e + 128
                    ]
                return carry

            lax.fori_loop(0, 4, body, 0, unroll=True)

    def piece(ref, r, kind):
        return ref[:, pl.ds(pl.multiple_of(r * 24 + kind * 8, 8), 8), :].reshape(256, 128)

    def put(ref, r, kind, value):
        ref[:, pl.ds(pl.multiple_of(r * 24 + kind * 8, 8), 8), :] = value.reshape(32, 8, 128)

    def lat_mix(pieces, orient, pairs):
        count = 3 if pairs is SIX else 2
        data = jnp.concatenate(pieces, axis=1)
        both = dots([lat_table[i] for i in range(count)], split(data, count), pairs)
        out = []
        for kind in range(3):
            direct_part = both[:256, 128 * kind : 128 * kind + 128]
            turned = both[256:, 128 * kind : 128 * kind + 128]
            out.append(direct_part + (orient * sign) * pltpu.roll(turned, 64, 1))
        return out

    def apply(pieces, layer, pairs, transposed):
        count = 3 if pairs is SIX else 2
        dims = ((1,), (1,)) if transposed else ((1,), (0,))
        parts = [split(value, count) for value in pieces]
        out = []
        for mode in range(2):
            left = [
                jnp.concatenate([parts[mode][i], parts[2][i]], axis=1) for i in range(count)
            ]
            right = [mats[layer * 2 + mode, i] for i in range(count)]
            out.append(dots(left, right, pairs, dims))
        return [out[0][:, :128], out[1][:, :128], out[0][:, 128:] + out[1][:, 128:]]

    def mat_grad(inputs, outputs, layer):
        left = [split(value, 2) for value in inputs]
        right = [split(value, 2) for value in outputs]
        for mode in range(2):
            lhs = [jnp.concatenate([left[mode][i], left[2][i]], axis=1) for i in range(2)]
            rhs = [jnp.concatenate([right[mode][i], right[2][i]], axis=1) for i in range(2)]
            mats_grad[layer * 2 + mode] += dots(lhs, rhs, THREE, ((0,), (0,)))
            total = jnp.concatenate([outputs[mode], outputs[2]], axis=1)
            sums_grad[layer * 2 + mode] += jnp.sum(total.reshape(32, 8, 256), axis=0)

    loads = []
    for i, (source, target) in enumerate(((fields, scaled), (cotangent, cot))):
        for g in range(3):
            loads.append(
                pltpu.make_async_copy(
                    source.at[g], target.at[pl.ds(g * STRIP, REAL)], io_sem.at[3 * i + g]
                )
            )
    pairs = (
        (turn_in, turn),
        (double_in, double),
        (plain_in, plain),
        (place_in, place),
        (place_t_in, place_t),
        (lat_in, lat_table),
        (back_plain_in, back_plain),
        (back_double_in, back_double),
    )
    tables = [
        pltpu.make_async_copy(source, target, table_sem.at[i])
        for i, (source, target) in enumerate(pairs)
    ]
    for copy in loads[:3]:
        copy.start()
    barrier = pltpu.get_barrier_semaphore()
    for d in range(1, 32):
        pl.semaphore_signal(
            barrier, inc=1, device_id=(lax.rem(me + d, 32), zed), device_id_type=MESH
        )
    for d in range(1, 4):
        pl.semaphore_signal(
            barrier, inc=1, device_id=(me, lax.rem(zed + d, 4)), device_id_type=MESH
        )
    for g in range(3):
        cot[pl.ds(g * STRIP + REAL, STRIP - REAL), :] = jnp.zeros((STRIP - REAL, 128), F32)
        scaled[pl.ds(g * STRIP + REAL, STRIP - REAL), :] = jnp.zeros((STRIP - REAL, 128), F32)
    for i, source in enumerate((gain, shift)):
        for g in range(3):
            value = source[:, 64 * g : 64 * g + 64]
            norm[3 * i + g : 3 * i + g + 1, :] = jnp.concatenate([value, value], axis=1)
    for copy in loads[:3]:
        copy.wait()
    for copy in tables[:2] + loads[3:] + tables[2:]:
        copy.start()

    def stats_body(k, carry):
        first = pl.multiple_of(k * PIECE, PIECE)
        rows = [scaled[pl.ds(g * STRIP + first, PIECE), :] for g in range(3)]
        here = token_sums(rows[0] + rows[1] + rows[2])
        mean = here * (1.0 / LOCAL)
        square = None
        for value in rows:
            centred = value - mean
            square = centred * centred if square is None else square + centred * centred
        zsend[0, 0, k] = pack(here)
        zsend[0, 1, k] = pack(token_sums(square))
        return carry

    lax.fori_loop(0, STRIP // PIECE, stats_body, 0, unroll=True)
    pl.semaphore_wait(barrier, 34)
    copies = exchange(0)

    def load_cot(g, h):
        return cot[pl.ds(g * STRIP + h, PADDED, stride=8), :]

    for copy in loads[3:] + tables[:2]:
        copy.wait()
    lon_forward(load_cot, double, THREE, send2, (0,))
    exchange_wait(0, copies)

    def norm_body(k, carry):
        sums = [zrecv[0, i, 0, k] for i in range(4)]
        squares = [zrecv[0, i, 1, k] for i in range(4)]
        mean = ((sums[0] + sums[1]) + (sums[2] + sums[3])) * (1.0 / EMBED)
        apart = None
        for value in sums:
            gap = value * (1.0 / LOCAL) - mean
            apart = gap * gap if apart is None else apart + gap * gap
        total = (squares[0] + squares[1]) + (squares[2] + squares[3]) + apart * LOCAL
        inverse = spread(lax.rsqrt(total * (1.0 / EMBED) + epsilon))
        mean = spread(mean)
        first = pl.multiple_of(k * PIECE, PIECE)
        inv[pl.ds(first, PIECE), :] = inverse
        for g in range(3):
            here = pl.ds(g * STRIP + first, PIECE)
            scaled[here, :] = (scaled[here, :] - mean) * inverse
        return carry

    lax.fori_loop(0, STRIP // PIECE, norm_body, 0, unroll=True)

    def load_normed(g, h):
        value = scaled[pl.ds(g * STRIP + h, PADDED, stride=8), :]
        return value * norm[g : g + 1] + norm[3 + g : 4 + g]

    tables[2].wait()
    lon_forward(load_normed, plain, SIX, send1, (0, 1))
    start(0, (0,))
    lon_forward(load_normed, plain, SIX, send1, (2,))
    start(0, (1,))
    lon_forward(load_cot, double, THREE, send2, (1, 2))

    for copy in tables[3:]:
        copy.wait()
    for layer, (weight, shifts) in enumerate(((weight1, bias1), (weight2, bias2))):
        for part in range(2):
            target = weights.at[layer * 2 + part]
            target[...] = jnp.zeros((128, 128), F32)
            for q in range(24):
                stage[q : q + 1, :] = weight[part, pl.ds(core, 1), 384 * q : 384 * q + 384]
            for t in range(4):
                value = stage[:, BLOCK * t : BLOCK * t + BLOCK]
                value = jnp.concatenate([value, jnp.zeros((24, 128 - BLOCK), F32)], axis=1)
                target[pl.ds(t, 24, stride=4), :] = value
            value = shifts[part, pl.ds(core, 1), :]
            target[BLOCK : BLOCK + 1, :BLOCK] = value
    for layer in range(2):
        for mode in range(2):
            to_real, to_imag = place[core, mode, 0], place[core, mode, 1]
            real = split(weights[layer * 2], 3)
            imag = split(weights[layer * 2 + 1], 3)

            def fan(parts, target):
                total = None
                for part in reversed(parts):
                    term = jnp.dot(part, target, preferred_element_type=F32)
                    total = term if total is None else total + term
                return total

            upper = fan(real, to_real) + fan(imag, to_imag)
            lower = fan(real, to_imag) - fan(imag, to_real)
            bias[layer * 2 + mode] = jnp.broadcast_to(upper[BLOCK : BLOCK + 1], (8, 256))

            def lift(source, value):
                total = None
                for part in reversed(split(value, 3)):
                    term = jnp.dot(source, part, preferred_element_type=F32)
                    total = term if total is None else total + term
                return total

            whole = lift(place_t[core, mode, 0], upper) + lift(place_t[core, mode, 1], lower)
            for i, part in enumerate(split(whole, 3)):
                mats[layer * 2 + mode, i] = part
    forward(0)
    start(1)

    def add_bias(pieces, layer):
        first, second = bias[layer * 2], bias[layer * 2 + 1]
        return [
            pieces[0] + first[0:1, :128],
            pieces[1] + second[0:1, :128],
            pieces[2] + (first[0:1, 128:] + second[0:1, 128:]),
        ]

    finish(0)

    def forward_body(r, carry):
        spectrum = lat_mix([piece(recv1, r, kind) for kind in range(3)], 1.0, SIX)
        for kind in range(3):
            put(recv1, r, kind, spectrum[kind])
        hidden = [jnp.maximum(v, 0.0) for v in add_bias(apply(spectrum, 0, SIX, False), 0)]
        for kind in range(3):
            put(act, r, kind, hidden[kind])
        out = add_bias(apply(hidden, 1, SIX, False), 1)
        out = [v - jnp.clip(v, -shrink_level, shrink_level) for v in out]
        for kind in range(3):
            put(shrunk, r, kind, out[kind])
        rows = lat_mix(out, -1.0, THREE)
        for kind in range(3):
            put(send3, r, kind, rows[kind])
        return carry

    forward(1)
    lax.fori_loop(0, EARLY, forward_body, 0)
    start(2)
    lax.fori_loop(EARLY, OWN, forward_body, 0)
    finish(1)

    mats_grad[...] = jnp.zeros_like(mats_grad)
    sums_grad[...] = jnp.zeros_like(sums_grad)

    def backward_body(r, carry):
        upstream = lat_mix([piece(recv2, r, kind) for kind in range(3)], 1.0, THREE)
        out_grad = [
            jnp.where(piece(shrunk, r, kind) != 0.0, upstream[kind], 0.0) for kind in range(3)
        ]
        hidden = [piece(act, r, kind) for kind in range(3)]
        mat_grad(hidden, out_grad, 1)
        hidden_grad = apply(out_grad, 1, THREE, True)
        pre_grad = [jnp.where(h > 0.0, g, 0.0) for h, g in zip(hidden, hidden_grad)]
        mat_grad([piece(recv1, r, kind) for kind in range(3)], pre_grad, 0)
        rows = lat_mix(apply(pre_grad, 0, THREE, True), -1.0, THREE)
        for kind in range(3):
            put(send4, r, kind, rows[kind])
        return carry

    lax.fori_loop(0, 2, backward_body, 0)
    forward(2)
    lax.fori_loop(2, EARLY, backward_body, 0)
    start(3)
    lax.fori_loop(EARLY, OWN, backward_body, 0)

    bias_row = lax.broadcasted_iota(jnp.int32, (128, 128), 0) == BLOCK
    for layer in range(2):
        real_total, imag_total = None, None
        for mode in range(2):
            real_t, imag_t = place_t[core, mode, 0], place_t[core, mode, 1]
            real_p, imag_p = place[core, mode, 0], place[core, mode, 1]
            grads = split(mats_grad[layer * 2 + mode], 2)
            to_real = sum(jnp.dot(v, real_t, preferred_element_type=F32) for v in grads)
            to_imag = sum(jnp.dot(v, imag_t, preferred_element_type=F32) for v in grads)

            def lower_to(target, value):
                return sum(
                    jnp.dot(target, v, preferred_element_type=F32) for v in split(value, 2)
                )

            real = lower_to(real_p, to_real) + lower_to(imag_p, to_imag)
            imag = lower_to(real_p, to_imag) - lower_to(imag_p, to_real)
            column = jnp.sum(sums_grad[layer * 2 + mode], axis=0, keepdims=True)
            column = jnp.broadcast_to(column, (16, 256))
            sums = split(column, 3)
            real_bias = sum(jnp.dot(v, real_t, preferred_element_type=F32) for v in sums)
            imag_bias = sum(jnp.dot(v, imag_t, preferred_element_type=F32) for v in sums)
            real = jnp.where(bias_row, real_bias[0:1], real)
            imag = jnp.where(bias_row, imag_bias[0:1], imag)
            real_total = real if real_total is None else real_total + real
            imag_total = imag if imag_total is None else imag_total + imag
        for part, value in enumerate((real_total, imag_total)):
            weights[layer * 2 + part] = value
    for i in range(4):
        columns = [
            weights[i, pl.ds(t, QUARTER, stride=4), :][:, :BLOCK] for t in range(4)
        ]
        part_send[pl.ds(i * QUARTER, QUARTER), :] = jnp.concatenate(columns, axis=1)
    row = jnp.concatenate([weights[i, BLOCK : BLOCK + 1, :][:, :BLOCK] for i in range(4)], axis=1)
    top = lax.broadcasted_iota(jnp.int32, (8, WIDE), 0) == 0
    part_send[pl.ds(4 * QUARTER, 8), :] = jnp.where(top, row, 0.0)

    def part_copy(d):
        other = lax.rem(chip + d, 16)
        return other, remote(
            part_send.at[pl.ds(lax.rem(other, PARTS) * PART, PART)],
            part_recv.at[chip],
            p_ssem.at[d],
            p_rsem.at[chip],
            other * 2 + core,
        )

    for d in range(1, 16):
        other, copy = part_copy(d)
        pl.when(other < PARTS)(copy.start)
    part_recv[chip] = part_send[pl.ds(lax.rem(chip, PARTS) * PART, PART), :]
    forward(3)
    start(4)

    owner = chip < PARTS

    def sum_copy(d):
        other = lax.rem(chip + d, 16)
        return remote(
            part_sum,
            param_all.at[core, pl.ds(lax.rem(chip, PARTS) * PART, PART)],
            g_ssem.at[d],
            g_rsem.at[chip],
            other * 2 + core,
        )

    @pl.when(owner)
    def _():
        for d in range(1, 16):
            other = lax.rem(chip + d, 16)
            remote(
                part_send.at[pl.ds(0, PART)],
                part_recv.at[other],
                p_ssem.at[d],
                p_rsem.at[other],
                other * 2 + core,
            ).wait_recv()
        total = part_recv[0]
        for i in range(1, 16):
            total = total + part_recv[i]
        part_sum[...] = total * FACTOR
        param_all[core, pl.ds(lax.rem(chip, PARTS) * PART, PART), :] = total * FACTOR
        for d in range(1, 16):
            sum_copy(d).start()

    for n in range(3):
        drain(n)
    forward(4)
    start(5)

    for d in range(1, 16):
        other = lax.rem(chip + d, 16)
        copy = remote(
            part_sum,
            param_all.at[core, pl.ds(lax.rem(other, PARTS) * PART, PART)],
            g_ssem.at[d],
            g_rsem.at[other],
            other * 2 + core,
        )
        pl.when(other < PARTS)(copy.wait_recv)
    across = remote(
        param_all.at[core], param_all.at[core], c_sem.at[0], c_sem.at[1], index(y, x, 1 - core)
    )
    across.start()
    finish(3)
    finish(4)

    lon_inverse(recv4, back_plain, (0, 1, 2))

    def sums_body(k, gains):
        direct_sum, cross_sum = None, None
        gains = list(gains)
        first = pl.multiple_of(k * PIECE, PIECE)
        for g in range(3):
            here = pl.ds(g * STRIP + first, PIECE)
            normed_grad = cot[here, :] + result[here, :]
            unit = scaled[here, :]
            for slot, value in ((g, normed_grad * unit), (3 + g, normed_grad)):
                gains[slot] += jnp.sum(value.reshape(PIECE // 8, 8, 128), axis=0)
            scaled_grad = normed_grad * norm[g : g + 1]
            cot[here, :] = scaled_grad
            cross = scaled_grad * unit
            direct_sum = scaled_grad if direct_sum is None else direct_sum + scaled_grad
            cross_sum = cross if cross_sum is None else cross_sum + cross
        zsend[1, 0, k] = pack(token_sums(direct_sum))
        zsend[1, 1, k] = pack(token_sums(cross_sum))
        return tuple(gains)

    zero = jnp.zeros((8, 128), F32)
    gains = lax.fori_loop(0, STRIP // PIECE, sums_body, (zero,) * 6, unroll=True)
    copies = exchange(1)
    norm_rows = lax.broadcasted_iota(jnp.int32, (8, 128), 0)
    packed = jnp.zeros((8, 128), F32)
    for i, value in enumerate(gains):
        value = jnp.sum(value, axis=0, keepdims=True)
        packed = jnp.where(norm_rows == i, value, packed)
    norm_send[...] = packed + pltpu.roll(packed, 64, 1)
    norm_recv[me] = norm_send[...]

    def norm_copy(d):
        other = lax.rem(me + d, 32)
        return remote(norm_send, norm_recv.at[me], n_ssem.at[d], n_rsem.at[me], other)

    for d in range(1, 32):
        norm_copy(d).start()
    forward(5)
    exchange_wait(1, copies)

    def grad_body(k, carry):
        means = []
        for which in range(2):
            group = [zrecv[1, i, which, k] for i in range(4)]
            total = (group[0] + group[1]) + (group[2] + group[3])
            means.append(spread(total * (1.0 / EMBED)))
        first = pl.multiple_of(k * PIECE, PIECE)
        inverse = inv[pl.ds(first, PIECE), :]
        for g in range(3):
            here = pl.ds(g * STRIP + first, PIECE)
            cot[here, :] = inverse * (cot[here, :] - means[0] - scaled[here, :] * means[1])
        return carry

    lax.fori_loop(0, STRIP // PIECE, grad_body, 0, unroll=True)
    stores = []
    for g in range(3):
        stores.append(
            pltpu.make_async_copy(
                cot.at[pl.ds(g * STRIP, REAL)], grad_out.at[g], io_sem.at[3 + g]
            )
        )
        stores[-1].start()

    remote(
        param_all.at[1 - core],
        param_all.at[1 - core],
        c_sem.at[0],
        c_sem.at[1],
        index(y, x, 1 - core),
    ).wait_recv()
    across.wait_send()
    param_out[...] = param_all[...]
    for d in range(1, 32):
        other = lax.rem(me + d, 32)
        remote(
            norm_send, norm_recv.at[other], n_ssem.at[d], n_rsem.at[other], other
        ).wait_recv()
        norm_copy(d).wait_send()
    total = norm_recv[0]
    for i in range(1, 32):
        total = total + norm_recv[i]
    norm_out[...] = total * FACTOR
    for d in range(1, 16):
        other, copy = part_copy(d)
        pl.when(other < PARTS)(copy.wait_send)

    @pl.when(owner)
    def _():
        for d in range(1, 16):
            sum_copy(d).wait_send()

    drain(3)
    drain(4)

    finish(2)
    finish(5)
    for g in range(3):
        lon_inverse(recv3, back_double, (g,))
        here = pl.ds(g * STRIP, REAL)
        result[here, :] = (
            result[here, :] + scaled[here, :] * norm[g : g + 1] + norm[3 + g : 4 + g]
        )
        stores.append(
            pltpu.make_async_copy(
                result.at[pl.ds(g * STRIP, REAL)], mixed_out.at[g], io_sem.at[g]
            )
        )
        stores[-1].start()
    drain(5)
    for copy in stores:
        copy.wait()


def finisher(
    mixed,
    grad,
    params,
    norms,
    mixed_out,
    grad_out,
    gain_out,
    shift_out,
    weight1_out,
    bias1_out,
    weight2_out,
    bias2_out,
    held,
    sem,
):
    loads, stores = [], []
    for i, (source, target) in enumerate(((mixed, mixed_out), (grad, grad_out))):
        for g in range(3):
            for part in range(3):
                n = 9 * i + 3 * g + part
                here = pl.ds(part * (REAL // 3), REAL // 3)
                there = held.at[3 * i + g, here]
                loads.append(pltpu.make_async_copy(source.at[g, here], there, sem.at[n]))
                stores.append(pltpu.make_async_copy(there, target.at[g, here], sem.at[18 + n]))
                loads[-1].start()
    for load, store in zip(loads, stores):
        load.wait()
        store.start()
    gain_out[...] = jnp.concatenate([norms[g : g + 1, :64] for g in range(3)], axis=1)
    shift_out[...] = jnp.concatenate([norms[3 + g : 4 + g, :64] for g in range(3)], axis=1)
    for layer, (weight, shifts) in enumerate(
        ((weight1_out, bias1_out), (weight2_out, bias2_out))
    ):
        for part in range(2):
            i = layer * 2 + part
            for half in range(2):
                for q in range(QUARTER):
                    row = i * QUARTER + q
                    weight[part, half : half + 1, WIDE * q : WIDE * q + WIDE] = params[
                        half, row : row + 1, :
                    ]
                row = params[half, 4 * QUARTER : 4 * QUARTER + 1, :]
                shifts[part, half : half + 1, :] = row[:, BLOCK * i : BLOCK * i + BLOCK]
    for store in stores:
        store.wait()


def shards(
    fields, cotangent, norm_gain, norm_shift, first_weight, first_bias, second_weight, second_bias
):
    def rows(values):
        return values.reshape(8, 3, PAIRS, 128).transpose(1, 2, 0, 3).reshape(3, REAL, 128)

    def unrows(values):
        return values.reshape(3, PAIRS, 8, 128).transpose(2, 0, 1, 3).reshape(1, 8, 3, LON * 64)

    tables = make_tables()
    buffer = pltpu.VMEM((32, CHUNK, 128), F32)
    middle = pltpu.VMEM((18, CHUNK, 128), F32)
    strips = pltpu.VMEM((3 * STRIP, 128), F32)
    dma = pltpu.SemaphoreType.DMA
    vmem = pl.BlockSpec(memory_space=pltpu.VMEM)
    anywhere = pl.BlockSpec(memory_space=pl.ANY)
    wholes = (
        jax.ShapeDtypeStruct((3, REAL, 128), F32),
        jax.ShapeDtypeStruct((3, REAL, 128), F32),
    )
    middles = pl.pallas_call(
        kernel,
        out_shape=wholes
        + (
            jax.ShapeDtypeStruct((2, GRAD_ROWS, WIDE), F32),
            jax.ShapeDtypeStruct((8, 128), F32),
        ),
        in_specs=[anywhere] * 2 + [vmem] * 6 + [anywhere] * 8 + [vmem],
        out_specs=[anywhere] * 2 + [vmem] * 2,
        scratch_shapes=[pltpu.VMEM(table.shape, table.dtype) for table in tables[:8]]
        + [
            strips,
            strips,
            pltpu.VMEM((STRIP, 128), F32),
            strips,
        ]
        + [buffer] * 8
        + [middle] * 4
        + [
            buffer,
            buffer,
            pltpu.VMEM((4, 3, 256, 256), BF16),
            pltpu.VMEM((4, 256, 256), F32),
            pltpu.VMEM((4, 8, 256), F32),
            pltpu.VMEM((4, 8, 256), F32),
            pltpu.VMEM((8, 128), F32),
            pltpu.VMEM((4, 128, 128), F32),
            pltpu.VMEM((24, 384), F32),
            pltpu.VMEM((2, 2, STRIP // PIECE, 8, 128), F32),
            pltpu.VMEM((2, 4, 2, STRIP // PIECE, 8, 128), F32),
            pltpu.VMEM((GRAD_ROWS, WIDE), F32),
            pltpu.VMEM((16, PART, WIDE), F32),
            pltpu.VMEM((PART, WIDE), F32),
            pltpu.VMEM((2, GRAD_ROWS, WIDE), F32),
            pltpu.VMEM((8, 128), F32),
            pltpu.VMEM((32, 8, 128), F32),
            dma((6,)),
            dma((8,)),
            dma((2, 4)),
            dma((2, 4)),
            dma((6, 49)),
            dma((6, 32)),
            dma((6, 18)),
            dma((16,)),
            dma((16,)),
            dma((16,)),
            dma((16,)),
            dma((2,)),
            dma((32,)),
            dma((32,)),
        ],
        compiler_params=pltpu.CompilerParams(
            collective_id=1, has_side_effects=True, vmem_limit_bytes=63 * 2**20
        ),
        cost_estimate=pl.CostEstimate(
            flops=5_500_000_000, bytes_accessed=12_000_000, transcendentals=0
        ),
        name="mixer",
    )(
        rows(fields),
        rows(cotangent),
        norm_gain.reshape(1, LOCAL),
        norm_shift.reshape(1, LOCAL),
        first_weight,
        first_bias,
        second_weight,
        second_bias,
        *tables,
    )
    mixed, grad, *rest = pl.pallas_call(
        finisher,
        out_shape=wholes
        + (
            jax.ShapeDtypeStruct((1, LOCAL), F32),
            jax.ShapeDtypeStruct((1, LOCAL), F32),
            jax.ShapeDtypeStruct(first_weight.shape, F32),
            jax.ShapeDtypeStruct(first_bias.shape, F32),
            jax.ShapeDtypeStruct(second_weight.shape, F32),
            jax.ShapeDtypeStruct(second_bias.shape, F32),
        ),
        in_specs=[anywhere] * 2 + [vmem] * 2,
        out_specs=[anywhere] * 2 + [vmem] * 6,
        scratch_shapes=[pltpu.VMEM((6, REAL, 128), F32), dma((36,))],
        compiler_params=pltpu.CompilerParams(vmem_limit_bytes=63 * 2**20),
        name="finisher",
    )(*middles)
    return (unrows(mixed), unrows(grad), rest[0].reshape(LOCAL), rest[1].reshape(LOCAL), *rest[2:])


def solution(mesh):
    big = P(None, "lat", "chan", None)
    small = P(None, "chan", None)
    return jax.shard_map(
        shards,
        mesh=mesh,
        in_specs=(big, big, P("chan"), P("chan"), small, small, small, small),
        out_specs=(big, big, P("chan"), P("chan"), small, small, small, small),
        check_vma=False,
    )
```

```python
import functools
import math

import jax
import jax.numpy as jnp
import ml_dtypes
import numpy as np
from jax import lax
from jax.experimental import pallas as pl
from jax.experimental.pallas import tpu as pltpu
from jax.sharding import PartitionSpec as P

F32 = jnp.float32
BF16 = jnp.bfloat16
MESH = pl.DeviceIdType.MESH

LON = 450
EMBED = 768
LOCAL = 192
BLOCK = 96
PAIRS = 225
PADDED = 240
STRIP = PADDED * 8
REAL = PAIRS * 8
RANK = 112
TALL = 120
OWN = 7
KINDS = 3
CHUNK = OWN * KINDS * 8
PIECE = 384
WIDE = 4 * BLOCK
QUARTER = BLOCK // 4
GRAD_ROWS = 4 * QUARTER + 8
PART = 8
PARTS = GRAD_ROWS // PART
EARLY = 4

epsilon = 1e-05
shrink_level = 0.05

SIX = ((1, 1), (0, 2), (2, 0), (0, 1), (1, 0), (0, 0))
THREE = ((0, 1), (1, 0), (0, 0))
FACTOR = 1.0 / math.sqrt(256 * LON)


def split_table(values, count):
    parts = []
    rest = values.astype(np.float64)
    for _ in range(count):
        part = rest.astype(np.float32).astype(ml_dtypes.bfloat16)
        parts.append(part)
        rest = rest - part.astype(np.float64)
    return np.stack(parts)


def make_tables():
    order = np.array([0] + list(range(2, 113)) + [1])
    places = np.arange(PAIRS)
    angles = 2.0 * np.pi * (order[:, None] * places[None, :] % PAIRS) / PAIRS
    plain = np.zeros((PADDED, PADDED))
    plain[: len(order), :PAIRS] = np.cos(angles) / np.sqrt(LON)
    plain[TALL : TALL + len(order), :PAIRS] = -np.sin(angles) / np.sqrt(LON)
    scale = np.full(TALL, 2.0)
    scale[0] = 1.0
    double = plain * np.concatenate([scale, scale])[:, None]
    turn = np.zeros((2, TALL, 128), np.float32)
    turn[0, :, :64] = 1.0
    turn[0, : len(order), 64:] = np.cos(2.0 * np.pi * order / LON)[:, None]
    turn[1, : len(order), 64:] = np.sin(2.0 * np.pi * order / LON)[:, None]
    rows = np.arange(256)
    lat_angles = 2.0 * np.pi * (rows[:, None] * rows[None, :] % 256) / 256
    lat = np.concatenate([np.cos(lat_angles), np.sin(lat_angles)]) / 16.0
    place = np.zeros((2, 2, 2, 128, 256), np.float32)
    for core in range(2):
        for mode in range(2):
            for part in range(2):
                for i in range(BLOCK):
                    in_shared = i >= 64 if core == 0 else i < 32
                    if in_shared:
                        lane = 128 + 64 * part + 32 * mode + i % 32
                    else:
                        lane = 64 * part + (i if core == 0 else i - 32)
                    place[core, mode, part, i, lane] = 1.0
    ones = np.kron(np.eye(2), np.ones((64, 64)))
    bf = ml_dtypes.bfloat16
    return (
        split_table(plain, 3),
        split_table(double, 2),
        split_table(plain.T, 2),
        split_table(double.T, 2),
        split_table(lat, 3),
        turn,
        place.astype(bf),
        np.swapaxes(place, -1, -2).astype(bf),
        ones.astype(bf),
    )


def split(value, count):
    parts = []
    for _ in range(count):
        part = value.astype(BF16)
        parts.append(part)
        value = value - part.astype(F32)
    return parts


def dots(left, right, pairs, dims=((1,), (0,))):
    total = None
    for i, j in pairs:
        term = lax.dot_general(left[i], right[j], (dims, ((), ())), preferred_element_type=F32)
        total = term if total is None else total + term
    return total


def kernel(
    fields,
    cotangent,
    gain,
    shift,
    weight1,
    bias1,
    weight2,
    bias2,
    plain_in,
    double_in,
    back_plain_in,
    back_double_in,
    lat_in,
    turn_in,
    place_in,
    place_t_in,
    ones,
    mixed_out,
    grad_out,
    param_out,
    norm_out,
    plain,
    double,
    back_plain,
    back_double,
    lat_table,
    turn,
    place,
    place_t,
    scaled,
    cot,
    inv,
    result,
    send1,
    send2,
    send3,
    send4,
    recv1,
    recv2,
    recv3,
    recv4,
    mid1,
    mid2,
    mid3,
    mid4,
    act,
    shrunk,
    mats,
    mats_grad,
    sums_grad,
    bias,
    norm,
    weights,
    stage,
    zsend,
    zrecv,
    part_send,
    part_recv,
    part_sum,
    param_all,
    norm_send,
    norm_recv,
    io_sem,
    table_sem,
    z_ssem,
    z_rsem,
    s_sem,
    r_sem,
    m_sem,
    p_ssem,
    p_rsem,
    g_ssem,
    g_rsem,
    c_sem,
    n_ssem,
    n_rsem,
):
    me = lax.axis_index("lat")
    zed = lax.axis_index("chan")
    y, x, core = me // 8, (me // 2) % 4, me % 2
    chip = y * 4 + x
    lane = lax.broadcasted_iota(jnp.int32, (1, 128), 1)
    low = lane < 64
    low32 = lane % 64 < 32
    sign = jnp.where(low, 1.0, -1.0).astype(F32)

    sends = (send1, send2, send3, send4, send4, send3)
    recvs = (recv1, recv2, recv3, recv4, recv4, recv3)
    mids = (mid1, mid2, mid3, mid4, mid4, mid3)
    spans = ((0, OWN), (0, OWN), (0, EARLY), (0, EARLY), (EARLY, OWN), (EARLY, OWN))

    def at(dy, dx):
        return lax.rem(y + dy, 4), lax.rem(x + dx, 4)

    def index(row, column, half):
        return (row * 4 + column) * 2 + half

    def row_slot(row, column, half):
        return half * 16 + row * 4 + column

    def slots(n):
        return (row_slot, index) if n < 2 else (index, row_slot)

    direct = [(0, 0, 2)] + [(0, d, k) for d in (1, 3, 2) for k in (0, 1)]
    direct += [(d, 0, k) for d in (1, 3, 2) for k in (0, 1)]
    latin = [(1, 1), (3, 3), (2, 2), (1, 3), (3, 2), (2, 1), (1, 2), (3, 1), (2, 3)]
    corner = [(dy, dx, k) for dy, dx in latin for k in (0, 1)]

    def corner_slot(dy, dx, k):
        return k * 9 + (dy - 1) * 3 + dx - 1

    def remote(src, dst, ssem, rsem, device):
        return pltpu.make_async_remote_copy(
            src_ref=src,
            dst_ref=dst,
            send_sem=ssem,
            recv_sem=rsem,
            device_id=(device, zed),
            device_id_type=MESH,
        )

    def chunk(n, ref, slot):
        first, last = spans[n]
        return ref.at[slot, pl.ds(24 * first, 24 * (last - first))]

    def first_leg(n, i):
        dy, dx, k = corner[i]
        row, column = at(dy, dx)
        src_slot = slots(n)[0](row, column, k)
        slot = corner_slot(dy, dx, k)
        device = index(y, column, core) if k == 0 else index(row, x, core)
        return remote(
            chunk(n, sends[n], src_slot),
            chunk(n, mids[n], slot),
            s_sem.at[n, i],
            m_sem.at[n, slot],
            device,
        )

    def second_leg(n, i):
        dy, dx, k = corner[i]
        slot = corner_slot(dy, dx, k)
        if k == 0:
            origin = (y, lax.rem(x + 4 - dx, 4))
            final = (lax.rem(y + dy, 4), x)
        else:
            origin = (lax.rem(y + 4 - dy, 4), x)
            final = (y, lax.rem(x + dx, 4))
        return remote(
            chunk(n, mids[n], slot),
            chunk(n, recvs[n], slots(n)[1](origin[0], origin[1], core)),
            s_sem.at[n, 18 + i],
            r_sem.at[n, index(origin[0], origin[1], core)],
            index(final[0], final[1], k),
        )

    def direct_leg(n, i):
        dy, dx, k = direct[i]
        half = 1 - core if k == 2 else k
        row, column = at(dy, dx)
        return remote(
            chunk(n, sends[n], slots(n)[0](row, column, half)),
            chunk(n, recvs[n], slots(n)[1](y, x, core)),
            s_sem.at[n, 36 + i],
            r_sem.at[n, me],
            index(row, column, half),
        )

    def start(n, halves=(0, 1)):
        for i in range(18):
            if corner[i][2] in halves:
                first_leg(n, i).start()
        for i in range(1, 13):
            if direct[i][2] in halves:
                direct_leg(n, i).start()
        if 1 in halves:
            direct_leg(n, 0).start()
            mine = slots(n)[0](y, x, core)
            theirs = slots(n)[1](y, x, core)
            here = pl.ds(24 * spans[n][0], 24 * (spans[n][1] - spans[n][0]))
            recvs[n][theirs, here] = sends[n][mine, here]

    def forward(n, first=0, last=18):
        for i in range(first, last):
            first_leg(n, i).wait_recv()
            second_leg(n, i).start()

    def finish(n):
        for d in range(1, 32):
            origin = lax.rem(me + d, 32)
            slot = slots(n)[1](origin // 8, (origin // 2) % 4, origin % 2)
            remote(
                chunk(n, sends[n], 0), chunk(n, recvs[n], slot), s_sem.at[n, 0], r_sem.at[n, origin], origin
            ).wait_recv()

    def drain(n):
        for i in range(18):
            first_leg(n, i).wait_send()
            second_leg(n, i).wait_send()
        for i in range(13):
            direct_leg(n, i).wait_send()

    def exchange(stage):
        copies = []
        for d in range(1, 4):
            other = lax.rem(zed + d, 4)
            copies.append(
                pltpu.make_async_remote_copy(
                    src_ref=zsend.at[stage],
                    dst_ref=zrecv.at[stage, zed],
                    send_sem=z_ssem.at[stage, d],
                    recv_sem=z_rsem.at[stage, zed],
                    device_id=(me, other),
                    device_id_type=MESH,
                )
            )
        for copy in copies:
            copy.start()
        zrecv[stage, zed] = zsend[stage]
        return copies

    def exchange_wait(stage, copies):
        for copy in copies:
            copy.wait_send()
        for d in range(1, 4):
            other = lax.rem(zed + d, 4)
            pltpu.make_async_remote_copy(
                src_ref=zsend.at[stage],
                dst_ref=zrecv.at[stage, other],
                send_sem=z_ssem.at[stage, d],
                recv_sem=z_rsem.at[stage, other],
                device_id=(me, other),
                device_id_type=MESH,
            ).wait_recv()

    lane48 = lax.broadcasted_iota(jnp.int32, (48, 8, 128), 2) % 64
    own_lane = lane48 == lax.broadcasted_iota(jnp.int32, (48, 8, 128), 0)

    def token_sums(value):
        total = None
        for part in reversed(split(value, 3)):
            term = jnp.dot(part, ones[...], preferred_element_type=F32)
            total = term if total is None else total + term
        return total

    def pack(value):
        return jnp.sum(jnp.where(own_lane, value.reshape(48, 8, 128), 0.0), axis=0)

    def spread(rows):
        return token_sums(jnp.where(own_lane, rows[None], 0.0).reshape(PIECE, 128))

    def lon_forward(load, table, pairs, out, groups):
        count = 3 if pairs is SIX else 2
        flat = out.reshape(32 * CHUNK, 128)
        cos_turn, sin_turn = turn[0], turn[1]
        top = lax.broadcasted_iota(jnp.int32, (TALL, 128), 0) == 0
        for g in groups:

            def body(step, carry, g=g):
                h0 = step * 2
                data = jnp.concatenate([load(g, h0), load(g, h0 + 1)], axis=1)
                parts = split(data, count)
                both = dots([table[i] for i in range(count)], parts, pairs)
                for e in range(2):
                    real = both[:TALL, 128 * e : 128 * e + 128]
                    imag = both[TALL:, 128 * e : 128 * e + 128]
                    turned_real = real * cos_turn + imag * sin_turn
                    turned_imag = imag * cos_turn - real * sin_turn
                    even = jnp.where(low, turned_real, pltpu.roll(turned_imag, 64, 1))
                    odd = jnp.where(low, pltpu.roll(turned_real, 64, 1), turned_imag)
                    a = even + odd
                    b = (even - odd) * sign
                    b = jnp.where(top, a[RANK : RANK + 1], b)
                    h = h0 + e

                    def store(half, kind, value):
                        flat[pl.ds(half * 16 * CHUNK + kind * 8 + h, RANK, stride=24), :] = value[
                            :RANK
                        ]

                    if g == 1:
                        store(0, 2, jnp.where(low32, a, pltpu.roll(b, 32, 1)))
                        store(1, 2, jnp.where(low32, pltpu.roll(a, 96, 1), b))
                    else:
                        store(g // 2, 0, a)
                        store(g // 2, 1, b)
                return carry

            lax.fori_loop(0, 4, body, 0, unroll=True)

    def lon_inverse(source, table, groups):
        flat = source.reshape(32 * CHUNK, 128)
        cos_turn, sin_turn = turn[0], turn[1]
        top = lax.broadcasted_iota(jnp.int32, (RANK, 128), 0) == 0
        top8 = lax.broadcasted_iota(jnp.int32, (8, 128), 0) == 0
        for g in groups:

            def body(step, carry, g=g):
                h0 = step * 2
                columns = []
                for e in range(2):
                    h = h0 + e

                    def fetch(half, kind):
                        return flat[pl.ds(half * 16 * CHUNK + kind * 8 + h, RANK, stride=24), :]

                    if g == 1:
                        u0, u1 = fetch(0, 2), fetch(1, 2)
                        a = jnp.where(low32, u0, pltpu.roll(u1, 32, 1))
                        b = jnp.where(low32, pltpu.roll(u0, 96, 1), u1)
                    else:
                        a, b = fetch(g // 2, 0), fetch(g // 2, 1)
                    last = jnp.where(top8, b[0:1], 0.0)
                    b = jnp.where(top, 0.0, b * sign)
                    even = jnp.concatenate([a + b, last], axis=0)
                    odd = jnp.concatenate([a - b, last], axis=0)
                    real = jnp.where(low, even, pltpu.roll(odd, 64, 1))
                    imag = jnp.where(low, pltpu.roll(even, 64, 1), odd)
                    turned_real = real * cos_turn - imag * sin_turn
                    turned_imag = imag * cos_turn + real * sin_turn
                    columns.append(jnp.concatenate([turned_real, turned_imag], axis=0))
                data = jnp.concatenate(columns, axis=1)
                out = dots([table[0], table[1]], split(data, 2), THREE)
                for e in range(2):
                    result[pl.ds(g * STRIP + h0 + e, PADDED, stride=8), :] = out[
                        :, 128 * e : 128 * e + 128
                    ]
                return carry

            lax.fori_loop(0, 4, body, 0, unroll=True)

    def piece(ref, r, kind):
        return ref[:, pl.ds(pl.multiple_of(r * 24 + kind * 8, 8), 8), :].reshape(256, 128)

    def put(ref, r, kind, value):
        ref[:, pl.ds(pl.multiple_of(r * 24 + kind * 8, 8), 8), :] = value.reshape(32, 8, 128)

    def lat_mix(pieces, orient, pairs):
        count = 3 if pairs is SIX else 2
        data = jnp.concatenate(pieces, axis=1)
        both = dots([lat_table[i] for i in range(count)], split(data, count), pairs)
        out = []
        for kind in range(3):
            direct_part = both[:256, 128 * kind : 128 * kind + 128]
            turned = both[256:, 128 * kind : 128 * kind + 128]
            out.append(direct_part + (orient * sign) * pltpu.roll(turned, 64, 1))
        return out

    def apply(pieces, layer, pairs, transposed):
        count = 3 if pairs is SIX else 2
        dims = ((1,), (1,)) if transposed else ((1,), (0,))
        parts = [split(value, count) for value in pieces]
        out = []
        for mode in range(2):
            left = [
                jnp.concatenate([parts[mode][i], parts[2][i]], axis=1) for i in range(count)
            ]
            right = [mats[layer * 2 + mode, i] for i in range(count)]
            out.append(dots(left, right, pairs, dims))
        return [out[0][:, :128], out[1][:, :128], out[0][:, 128:] + out[1][:, 128:]]

    def mat_grad(inputs, outputs, layer):
        left = [split(value, 2) for value in inputs]
        right = [split(value, 2) for value in outputs]
        for mode in range(2):
            lhs = [jnp.concatenate([left[mode][i], left[2][i]], axis=1) for i in range(2)]
            rhs = [jnp.concatenate([right[mode][i], right[2][i]], axis=1) for i in range(2)]
            mats_grad[layer * 2 + mode] += dots(lhs, rhs, THREE, ((0,), (0,)))
            total = jnp.concatenate([outputs[mode], outputs[2]], axis=1)
            sums_grad[layer * 2 + mode] += jnp.sum(total.reshape(32, 8, 256), axis=0)

    loads = []
    for i, (source, target) in enumerate(((fields, scaled), (cotangent, cot))):
        for g in range(3):
            loads.append(
                pltpu.make_async_copy(
                    source.at[g], target.at[pl.ds(g * STRIP, REAL)], io_sem.at[3 * i + g]
                )
            )
    pairs = (
        (turn_in, turn),
        (double_in, double),
        (plain_in, plain),
        (place_in, place),
        (place_t_in, place_t),
        (lat_in, lat_table),
        (back_plain_in, back_plain),
        (back_double_in, back_double),
    )
    tables = [
        pltpu.make_async_copy(source, target, table_sem.at[i])
        for i, (source, target) in enumerate(pairs)
    ]
    for copy in loads[:3]:
        copy.start()
    barrier = pltpu.get_barrier_semaphore()
    for d in range(1, 32):
        pl.semaphore_signal(
            barrier, inc=1, device_id=(lax.rem(me + d, 32), zed), device_id_type=MESH
        )
    for d in range(1, 4):
        pl.semaphore_signal(
            barrier, inc=1, device_id=(me, lax.rem(zed + d, 4)), device_id_type=MESH
        )
    for g in range(3):
        cot[pl.ds(g * STRIP + REAL, STRIP - REAL), :] = jnp.zeros((STRIP - REAL, 128), F32)
        scaled[pl.ds(g * STRIP + REAL, STRIP - REAL), :] = jnp.zeros((STRIP - REAL, 128), F32)
    for i, source in enumerate((gain, shift)):
        for g in range(3):
            value = source[:, 64 * g : 64 * g + 64]
            norm[3 * i + g : 3 * i + g + 1, :] = jnp.concatenate([value, value], axis=1)
    for copy in loads[:3]:
        copy.wait()
    for copy in tables[:2] + loads[3:] + tables[2:]:
        copy.start()

    def stats_body(k, carry):
        first = pl.multiple_of(k * PIECE, PIECE)
        rows = [scaled[pl.ds(g * STRIP + first, PIECE), :] for g in range(3)]
        here = token_sums(rows[0] + rows[1] + rows[2])
        mean = here * (1.0 / LOCAL)
        square = None
        for value in rows:
            centred = value - mean
            square = centred * centred if square is None else square + centred * centred
        zsend[0, 0, k] = pack(here)
        zsend[0, 1, k] = pack(token_sums(square))
        return carry

    lax.fori_loop(0, STRIP // PIECE, stats_body, 0, unroll=True)
    pl.semaphore_wait(barrier, 34)
    copies = exchange(0)

    def load_cot(g, h):
        return cot[pl.ds(g * STRIP + h, PADDED, stride=8), :]

    for copy in loads[3:] + tables[:2]:
        copy.wait()
    lon_forward(load_cot, double, THREE, send2, (0,))
    exchange_wait(0, copies)

    def norm_body(k, carry):
        sums = [zrecv[0, i, 0, k] for i in range(4)]
        squares = [zrecv[0, i, 1, k] for i in range(4)]
        mean = ((sums[0] + sums[1]) + (sums[2] + sums[3])) * (1.0 / EMBED)
        apart = None
        for value in sums:
            gap = value * (1.0 / LOCAL) - mean
            apart = gap * gap if apart is None else apart + gap * gap
        total = (squares[0] + squares[1]) + (squares[2] + squares[3]) + apart * LOCAL
        inverse = spread(lax.rsqrt(total * (1.0 / EMBED) + epsilon))
        mean = spread(mean)
        first = pl.multiple_of(k * PIECE, PIECE)
        inv[pl.ds(first, PIECE), :] = inverse
        for g in range(3):
            here = pl.ds(g * STRIP + first, PIECE)
            scaled[here, :] = (scaled[here, :] - mean) * inverse
        return carry

    lax.fori_loop(0, STRIP // PIECE, norm_body, 0, unroll=True)

    def load_normed(g, h):
        value = scaled[pl.ds(g * STRIP + h, PADDED, stride=8), :]
        return value * norm[g : g + 1] + norm[3 + g : 4 + g]

    tables[2].wait()
    lon_forward(load_normed, plain, SIX, send1, (0, 1))
    start(0, (0,))
    lon_forward(load_normed, plain, SIX, send1, (2,))
    start(0, (1,))
    lon_forward(load_cot, double, THREE, send2, (1, 2))

    for copy in tables[3:]:
        copy.wait()
    for layer, (weight, shifts) in enumerate(((weight1, bias1), (weight2, bias2))):
        for part in range(2):
            target = weights.at[layer * 2 + part]
            target[...] = jnp.zeros((128, 128), F32)
            for q in range(24):
                stage[q : q + 1, :] = weight[part, pl.ds(core, 1), 384 * q : 384 * q + 384]
            for t in range(4):
                value = stage[:, BLOCK * t : BLOCK * t + BLOCK]
                value = jnp.concatenate([value, jnp.zeros((24, 128 - BLOCK), F32)], axis=1)
                target[pl.ds(t, 24, stride=4), :] = value
            value = shifts[part, pl.ds(core, 1), :]
            target[BLOCK : BLOCK + 1, :BLOCK] = value
    for layer in range(2):
        for mode in range(2):
            to_real, to_imag = place[core, mode, 0], place[core, mode, 1]
            real = split(weights[layer * 2], 3)
            imag = split(weights[layer * 2 + 1], 3)

            def fan(parts, target):
                total = None
                for part in reversed(parts):
                    term = jnp.dot(part, target, preferred_element_type=F32)
                    total = term if total is None else total + term
                return total

            upper = fan(real, to_real) + fan(imag, to_imag)
            lower = fan(real, to_imag) - fan(imag, to_real)
            bias[layer * 2 + mode] = jnp.broadcast_to(upper[BLOCK : BLOCK + 1], (8, 256))

            def lift(source, value):
                total = None
                for part in reversed(split(value, 3)):
                    term = jnp.dot(source, part, preferred_element_type=F32)
                    total = term if total is None else total + term
                return total

            whole = lift(place_t[core, mode, 0], upper) + lift(place_t[core, mode, 1], lower)
            for i, part in enumerate(split(whole, 3)):
                mats[layer * 2 + mode, i] = part
    forward(0)
    start(1)

    def add_bias(pieces, layer):
        first, second = bias[layer * 2], bias[layer * 2 + 1]
        return [
            pieces[0] + first[0:1, :128],
            pieces[1] + second[0:1, :128],
            pieces[2] + (first[0:1, 128:] + second[0:1, 128:]),
        ]

    finish(0)

    def forward_body(r, carry):
        spectrum = lat_mix([piece(recv1, r, kind) for kind in range(3)], 1.0, SIX)
        for kind in range(3):
            put(recv1, r, kind, spectrum[kind])
        hidden = [jnp.maximum(v, 0.0) for v in add_bias(apply(spectrum, 0, SIX, False), 0)]
        for kind in range(3):
            put(act, r, kind, hidden[kind])
        out = add_bias(apply(hidden, 1, SIX, False), 1)
        out = [v - jnp.clip(v, -shrink_level, shrink_level) for v in out]
        for kind in range(3):
            put(shrunk, r, kind, out[kind])
        rows = lat_mix(out, -1.0, THREE)
        for kind in range(3):
            put(send3, r, kind, rows[kind])
        return carry

    forward(1)
    lax.fori_loop(0, EARLY, forward_body, 0)
    start(2)
    lax.fori_loop(EARLY, OWN, forward_body, 0)
    finish(1)

    mats_grad[...] = jnp.zeros_like(mats_grad)
    sums_grad[...] = jnp.zeros_like(sums_grad)

    def backward_body(r, carry):
        upstream = lat_mix([piece(recv2, r, kind) for kind in range(3)], 1.0, THREE)
        out_grad = [
            jnp.where(piece(shrunk, r, kind) != 0.0, upstream[kind], 0.0) for kind in range(3)
        ]
        hidden = [piece(act, r, kind) for kind in range(3)]
        mat_grad(hidden, out_grad, 1)
        hidden_grad = apply(out_grad, 1, THREE, True)
        pre_grad = [jnp.where(h > 0.0, g, 0.0) for h, g in zip(hidden, hidden_grad)]
        mat_grad([piece(recv1, r, kind) for kind in range(3)], pre_grad, 0)
        rows = lat_mix(apply(pre_grad, 0, THREE, True), -1.0, THREE)
        for kind in range(3):
            put(send4, r, kind, rows[kind])
        return carry

    lax.fori_loop(0, 2, backward_body, 0)
    forward(2)
    lax.fori_loop(2, EARLY, backward_body, 0)
    start(3)
    lax.fori_loop(EARLY, OWN, backward_body, 0)

    bias_row = lax.broadcasted_iota(jnp.int32, (128, 128), 0) == BLOCK
    for layer in range(2):
        real_total, imag_total = None, None
        for mode in range(2):
            real_t, imag_t = place_t[core, mode, 0], place_t[core, mode, 1]
            real_p, imag_p = place[core, mode, 0], place[core, mode, 1]
            grads = split(mats_grad[layer * 2 + mode], 2)
            to_real = sum(jnp.dot(v, real_t, preferred_element_type=F32) for v in grads)
            to_imag = sum(jnp.dot(v, imag_t, preferred_element_type=F32) for v in grads)

            def lower_to(target, value):
                return sum(
                    jnp.dot(target, v, preferred_element_type=F32) for v in split(value, 2)
                )

            real = lower_to(real_p, to_real) + lower_to(imag_p, to_imag)
            imag = lower_to(real_p, to_imag) - lower_to(imag_p, to_real)
            column = jnp.sum(sums_grad[layer * 2 + mode], axis=0, keepdims=True)
            column = jnp.broadcast_to(column, (16, 256))
            sums = split(column, 3)
            real_bias = sum(jnp.dot(v, real_t, preferred_element_type=F32) for v in sums)
            imag_bias = sum(jnp.dot(v, imag_t, preferred_element_type=F32) for v in sums)
            real = jnp.where(bias_row, real_bias[0:1], real)
            imag = jnp.where(bias_row, imag_bias[0:1], imag)
            real_total = real if real_total is None else real_total + real
            imag_total = imag if imag_total is None else imag_total + imag
        for part, value in enumerate((real_total, imag_total)):
            weights[layer * 2 + part] = value
    for i in range(4):
        columns = [
            weights[i, pl.ds(t, QUARTER, stride=4), :][:, :BLOCK] for t in range(4)
        ]
        part_send[pl.ds(i * QUARTER, QUARTER), :] = jnp.concatenate(columns, axis=1)
    row = jnp.concatenate([weights[i, BLOCK : BLOCK + 1, :][:, :BLOCK] for i in range(4)], axis=1)
    top = lax.broadcasted_iota(jnp.int32, (8, WIDE), 0) == 0
    part_send[pl.ds(4 * QUARTER, 8), :] = jnp.where(top, row, 0.0)

    def part_copy(d):
        other = lax.rem(chip + d, 16)
        return other, remote(
            part_send.at[pl.ds(lax.rem(other, PARTS) * PART, PART)],
            part_recv.at[chip],
            p_ssem.at[d],
            p_rsem.at[chip],
            other * 2 + core,
        )

    for d in range(1, 16):
        other, copy = part_copy(d)
        pl.when(other < PARTS)(copy.start)
    part_recv[chip] = part_send[pl.ds(lax.rem(chip, PARTS) * PART, PART), :]
    forward(3)
    start(4)

    owner = chip < PARTS

    def sum_copy(d):
        other = lax.rem(chip + d, 16)
        return remote(
            part_sum,
            param_all.at[core, pl.ds(lax.rem(chip, PARTS) * PART, PART)],
            g_ssem.at[d],
            g_rsem.at[chip],
            other * 2 + core,
        )

    @pl.when(owner)
    def _():
        for d in range(1, 16):
            other = lax.rem(chip + d, 16)
            remote(
                part_send.at[pl.ds(0, PART)],
                part_recv.at[other],
                p_ssem.at[d],
                p_rsem.at[other],
                other * 2 + core,
            ).wait_recv()
        total = part_recv[0]
        for i in range(1, 16):
            total = total + part_recv[i]
        part_sum[...] = total * FACTOR
        param_all[core, pl.ds(lax.rem(chip, PARTS) * PART, PART), :] = total * FACTOR
        for d in range(1, 16):
            sum_copy(d).start()

    for n in range(3):
        drain(n)
    forward(4)
    start(5)

    for d in range(1, 16):
        other = lax.rem(chip + d, 16)
        copy = remote(
            part_sum,
            param_all.at[core, pl.ds(lax.rem(other, PARTS) * PART, PART)],
            g_ssem.at[d],
            g_rsem.at[other],
            other * 2 + core,
        )
        pl.when(other < PARTS)(copy.wait_recv)
    across = remote(
        param_all.at[core], param_all.at[core], c_sem.at[0], c_sem.at[1], index(y, x, 1 - core)
    )
    across.start()
    finish(3)
    finish(4)

    lon_inverse(recv4, back_plain, (0, 1, 2))

    def sums_body(k, gains):
        direct_sum, cross_sum = None, None
        gains = list(gains)
        first = pl.multiple_of(k * PIECE, PIECE)
        for g in range(3):
            here = pl.ds(g * STRIP + first, PIECE)
            normed_grad = cot[here, :] + result[here, :]
            unit = scaled[here, :]
            for slot, value in ((g, normed_grad * unit), (3 + g, normed_grad)):
                gains[slot] += jnp.sum(value.reshape(PIECE // 8, 8, 128), axis=0)
            scaled_grad = normed_grad * norm[g : g + 1]
            cot[here, :] = scaled_grad
            cross = scaled_grad * unit
            direct_sum = scaled_grad if direct_sum is None else direct_sum + scaled_grad
            cross_sum = cross if cross_sum is None else cross_sum + cross
        zsend[1, 0, k] = pack(token_sums(direct_sum))
        zsend[1, 1, k] = pack(token_sums(cross_sum))
        return tuple(gains)

    zero = jnp.zeros((8, 128), F32)
    gains = lax.fori_loop(0, STRIP // PIECE, sums_body, (zero,) * 6, unroll=True)
    copies = exchange(1)
    norm_rows = lax.broadcasted_iota(jnp.int32, (8, 128), 0)
    packed = jnp.zeros((8, 128), F32)
    for i, value in enumerate(gains):
        value = jnp.sum(value, axis=0, keepdims=True)
        packed = jnp.where(norm_rows == i, value, packed)
    norm_send[...] = packed + pltpu.roll(packed, 64, 1)
    norm_recv[me] = norm_send[...]

    def norm_copy(d):
        other = lax.rem(me + d, 32)
        return remote(norm_send, norm_recv.at[me], n_ssem.at[d], n_rsem.at[me], other)

    for d in range(1, 32):
        norm_copy(d).start()
    forward(5)
    exchange_wait(1, copies)

    def grad_body(k, carry):
        means = []
        for which in range(2):
            group = [zrecv[1, i, which, k] for i in range(4)]
            total = (group[0] + group[1]) + (group[2] + group[3])
            means.append(spread(total * (1.0 / EMBED)))
        first = pl.multiple_of(k * PIECE, PIECE)
        inverse = inv[pl.ds(first, PIECE), :]
        for g in range(3):
            here = pl.ds(g * STRIP + first, PIECE)
            cot[here, :] = inverse * (cot[here, :] - means[0] - scaled[here, :] * means[1])
        return carry

    lax.fori_loop(0, STRIP // PIECE, grad_body, 0, unroll=True)
    stores = []
    for g in range(3):
        stores.append(
            pltpu.make_async_copy(
                cot.at[pl.ds(g * STRIP, REAL)], grad_out.at[g], io_sem.at[3 + g]
            )
        )
        stores[-1].start()

    remote(
        param_all.at[1 - core],
        param_all.at[1 - core],
        c_sem.at[0],
        c_sem.at[1],
        index(y, x, 1 - core),
    ).wait_recv()
    across.wait_send()
    param_out[...] = param_all[...]
    for d in range(1, 32):
        other = lax.rem(me + d, 32)
        remote(
            norm_send, norm_recv.at[other], n_ssem.at[d], n_rsem.at[other], other
        ).wait_recv()
        norm_copy(d).wait_send()
    total = norm_recv[0]
    for i in range(1, 32):
        total = total + norm_recv[i]
    norm_out[...] = total * FACTOR
    for d in range(1, 16):
        other, copy = part_copy(d)
        pl.when(other < PARTS)(copy.wait_send)

    @pl.when(owner)
    def _():
        for d in range(1, 16):
            sum_copy(d).wait_send()

    drain(3)
    drain(4)

    finish(2)
    finish(5)
    for g in range(3):
        lon_inverse(recv3, back_double, (g,))
        here = pl.ds(g * STRIP, REAL)
        result[here, :] = (
            result[here, :] + scaled[here, :] * norm[g : g + 1] + norm[3 + g : 4 + g]
        )
        stores.append(
            pltpu.make_async_copy(
                result.at[pl.ds(g * STRIP, REAL)], mixed_out.at[g], io_sem.at[g]
            )
        )
        stores[-1].start()
    drain(5)
    for copy in stores:
        copy.wait()


def finisher(
    mixed,
    grad,
    params,
    norms,
    mixed_out,
    grad_out,
    gain_out,
    shift_out,
    weight1_out,
    bias1_out,
    weight2_out,
    bias2_out,
    sem,
):
    stores = []
    for i, (source, target) in enumerate(((mixed, mixed_out), (grad, grad_out))):
        for g in range(3):
            for part in range(3):
                n = 9 * i + 3 * g + part
                here = pl.ds(part * (REAL // 3), REAL // 3)
                stores.append(pltpu.make_async_copy(source.at[g, here], target.at[g, here], sem.at[18 + n]))
                stores[-1].start()
    gain_out[...] = jnp.concatenate([norms[g : g + 1, :64] for g in range(3)], axis=1)
    shift_out[...] = jnp.concatenate([norms[3 + g : 4 + g, :64] for g in range(3)], axis=1)
    for layer, (weight, shifts) in enumerate(
        ((weight1_out, bias1_out), (weight2_out, bias2_out))
    ):
        for part in range(2):
            i = layer * 2 + part
            for half in range(2):
                for q in range(QUARTER):
                    row = i * QUARTER + q
                    weight[part, half : half + 1, WIDE * q : WIDE * q + WIDE] = params[
                        half, row : row + 1, :
                    ]
                row = params[half, 4 * QUARTER : 4 * QUARTER + 1, :]
                shifts[part, half : half + 1, :] = row[:, BLOCK * i : BLOCK * i + BLOCK]
    for store in stores:
        store.wait()


def shards(
    fields, cotangent, norm_gain, norm_shift, first_weight, first_bias, second_weight, second_bias
):
    def rows(values):
        return values.reshape(8, 3, PAIRS, 128).transpose(1, 2, 0, 3).reshape(3, REAL, 128)

    def unrows(values):
        return values.reshape(3, PAIRS, 8, 128).transpose(2, 0, 1, 3).reshape(1, 8, 3, LON * 64)

    tables = make_tables()
    buffer = pltpu.VMEM((32, CHUNK, 128), F32)
    middle = pltpu.VMEM((18, CHUNK, 128), F32)
    strips = pltpu.VMEM((3 * STRIP, 128), F32)
    dma = pltpu.SemaphoreType.DMA
    vmem = pl.BlockSpec(memory_space=pltpu.VMEM)
    anywhere = pl.BlockSpec(memory_space=pl.ANY)
    wholes = (
        jax.ShapeDtypeStruct((3, REAL, 128), F32),
        jax.ShapeDtypeStruct((3, REAL, 128), F32),
    )
    inside = (pltpu.VMEM((3, REAL, 128), F32),) * 2
    middles = pl.pallas_call(
        kernel,
        out_shape=inside
        + (
            pltpu.VMEM((2, GRAD_ROWS, WIDE), F32),
            pltpu.VMEM((8, 128), F32),
        ),
        in_specs=[anywhere] * 2 + [vmem] * 6 + [anywhere] * 8 + [vmem],
        out_specs=[anywhere] * 2 + [vmem] * 2,
        scratch_shapes=[pltpu.VMEM(table.shape, table.dtype) for table in tables[:8]]
        + [
            strips,
            strips,
            pltpu.VMEM((STRIP, 128), F32),
            strips,
        ]
        + [buffer] * 8
        + [middle] * 4
        + [
            buffer,
            buffer,
            pltpu.VMEM((4, 3, 256, 256), BF16),
            pltpu.VMEM((4, 256, 256), F32),
            pltpu.VMEM((4, 8, 256), F32),
            pltpu.VMEM((4, 8, 256), F32),
            pltpu.VMEM((8, 128), F32),
            pltpu.VMEM((4, 128, 128), F32),
            pltpu.VMEM((24, 384), F32),
            pltpu.VMEM((2, 2, STRIP // PIECE, 8, 128), F32),
            pltpu.VMEM((2, 4, 2, STRIP // PIECE, 8, 128), F32),
            pltpu.VMEM((GRAD_ROWS, WIDE), F32),
            pltpu.VMEM((16, PART, WIDE), F32),
            pltpu.VMEM((PART, WIDE), F32),
            pltpu.VMEM((2, GRAD_ROWS, WIDE), F32),
            pltpu.VMEM((8, 128), F32),
            pltpu.VMEM((32, 8, 128), F32),
            dma((6,)),
            dma((8,)),
            dma((2, 4)),
            dma((2, 4)),
            dma((6, 49)),
            dma((6, 32)),
            dma((6, 18)),
            dma((16,)),
            dma((16,)),
            dma((16,)),
            dma((16,)),
            dma((2,)),
            dma((32,)),
            dma((32,)),
        ],
        compiler_params=pltpu.CompilerParams(
            collective_id=1, has_side_effects=True, vmem_limit_bytes=55 * 2**20
        ),
        cost_estimate=pl.CostEstimate(
            flops=5_500_000_000, bytes_accessed=12_000_000, transcendentals=0
        ),
        name="mixer",
    )(
        rows(fields),
        rows(cotangent),
        norm_gain.reshape(1, LOCAL),
        norm_shift.reshape(1, LOCAL),
        first_weight,
        first_bias,
        second_weight,
        second_bias,
        *tables,
    )
    mixed, grad, *rest = pl.pallas_call(
        finisher,
        out_shape=wholes
        + (
            jax.ShapeDtypeStruct((1, LOCAL), F32),
            jax.ShapeDtypeStruct((1, LOCAL), F32),
            jax.ShapeDtypeStruct(first_weight.shape, F32),
            jax.ShapeDtypeStruct(first_bias.shape, F32),
            jax.ShapeDtypeStruct(second_weight.shape, F32),
            jax.ShapeDtypeStruct(second_bias.shape, F32),
        ),
        in_specs=[anywhere] * 2 + [vmem] * 2,
        out_specs=[anywhere] * 2 + [vmem] * 6,
        scratch_shapes=[dma((36,))],
        compiler_params=pltpu.CompilerParams(vmem_limit_bytes=4 * 2**20),
        name="finisher",
    )(*middles)
    return (unrows(mixed), unrows(grad), rest[0].reshape(LOCAL), rest[1].reshape(LOCAL), *rest[2:])


def solution(mesh):
    big = P(None, "lat", "chan", None)
    small = P(None, "chan", None)
    return jax.shard_map(
        shards,
        mesh=mesh,
        in_specs=(big, big, P("chan"), P("chan"), small, small, small, small),
        out_specs=(big, big, P("chan"), P("chan"), small, small, small, small),
        check_vma=False,
    )
```
